32 devices in a mesh: row: 8 (over y, x, core), col: 4 (over z).
Axes of the slice: x: 2, y: 2, z: 4, core: 2. Of those that a mesh axis runs over, the one named last changes fastest.
Arguments:
- vectors: float32 [16384, 512], P(('row', 'col')), may hold values from -6 to 6
- panels: float32 [2, 16384, 256], P(None, 'row', 'col'), may hold values from -0.046875 to 0.046875
- tfactors: float32 [2, 256, 256], replicated, may hold values from -3 to 3, as said below
Outputs:
- transformed: float32 [16384, 512], P('row', 'col')
The draws below stay inside these ranges and needn't reach their ends.
Inputs may be any that keep to these rules, and one draw needn't show every extreme that they name: tfactors[p] is upper triangular with its diagonal between 1 and 2.
All inputs are finite; a program needn't handle non-finite values.
Results may differ from the reference program's by a relative error of at most 0.000071.
Values sent between devices are 32-bit elements; how exact they have to be, the bound alone decides.
No kernel may reach another device: no remote copies, remote signals or barrier semaphores. Data moves between devices by JAX's collectives and lax.ppermute only.
A program may use at most 64 MiB of HBM per device.

```python
import jax
import jax.numpy as jnp
from jax import lax

PANEL = 256
ORDER = 16384
EIGVECS = 512


def draw_tfactors(key, part):
    key = jax.random.fold_in(key, 7)
    key_diag, key_upper = jax.random.split(key)
    diag_vals = jax.random.uniform(key_diag, (2, PANEL), jnp.float32, 1.0, 2.0)
    upper = jax.random.normal(key_upper, (2, PANEL, PANEL), jnp.float32) * (0.5 / PANEL ** 0.5)
    upper = jnp.clip(upper, -3.0, 3.0)
    strict = jnp.triu(upper, 1)
    eye_mat = jnp.eye(PANEL, dtype=jnp.float32)
    return strict + eye_mat[None, :, :] * diag_vals[:, None, :]


def steps_of(stream_key, extent, pieces, low, largest):
    def one(position, parts):
        steps = jax.random.uniform(jax.random.fold_in(jax.random.fold_in(stream_key, 6), position), (parts,), jnp.float32, low / len(pieces), largest / len(pieces))
        return jnp.repeat(jnp.exp(steps), extent[position] // parts).reshape((-1,) + (1,) * (len(extent) - position - 1))

    loudness = one(*pieces[0])
    for cut in pieces[1:]:
        loudness = loudness * one(*cut)
    return loudness


def scatter_about(stream_key, dims, deviation, bound, cuts=(), kind=jnp.bfloat16):
    gain = steps_of(stream_key, dims, cuts, -0.22, 0.18) if cuts else 1.0
    result = jax.random.normal(stream_key, dims, jnp.float32) * deviation * gain
    return jnp.minimum(jnp.maximum(result, -bound), bound).astype(kind)


def setup_inputs(seed: int = 0) -> dict:
    keys = jax.random.split(jax.random.key(seed), 4)
    vectors = scatter_about(keys[0], (ORDER, EIGVECS), 1.0, 6.0, ((0, 32),), jnp.float32)
    panels = scatter_about(keys[1], (2, ORDER, PANEL), ORDER ** -0.5, 0.046875, ((1, 8), (2, 4)), jnp.float32)
    tfactors = draw_tfactors(jax.random.fold_in(keys[3], 71), 0)
    return dict(vectors=vectors, panels=panels, tfactors=tfactors)


def panel_product(panel, field):
    return lax.dot_general(panel, field, (((0,), (0,)), ((), ())), precision=lax.Precision.HIGHEST, preferred_element_type=jnp.float32)


def apply_panel(field, panel, factor):
    weights = panel_product(panel, field)
    scaled = jnp.dot(factor, weights, precision=lax.Precision.HIGHEST, preferred_element_type=jnp.float32)
    return field - jnp.dot(panel, scaled, precision=lax.Precision.HIGHEST, preferred_element_type=jnp.float32)


def reference(vectors, panels, tfactors):
    first = apply_panel(vectors, panels[0], tfactors[0])
    return apply_panel(first, panels[1], tfactors[1])
```

```python
import jax
import jax.numpy as jnp
from jax import lax
from jax.sharding import PartitionSpec as P


def matmul(left, right, contract):
    return lax.dot_general(
        left,
        right,
        (contract, ((), ())),
        precision=lax.Precision.HIGH,
        preferred_element_type=jnp.float32,
    )


def swap(block, axis, size, mask):
    return lax.ppermute(block, axis, [(i, i ^ mask) for i in range(size)])


def row_stages(size):
    stages = []
    shift = 0
    while (1 << shift) < size:
        bits = 1 if shift == 0 or (2 << shift) == size else 2
        stages.append((shift, 1 << bits))
        shift += bits
    return stages


def reduce_scatter_rows(partial, size):
    row = lax.axis_index("row")
    current = partial.reshape((size, partial.shape[0] // size, partial.shape[1]))
    for shift, group in row_stages(size):
        me = (row >> shift) & (group - 1)
        current = current.reshape((current.shape[0] // group, group) + current.shape[1:])
        pick = lambda k: lax.dynamic_index_in_dim(current, me ^ k, 1, keepdims=False)
        received = [swap(pick(k), "row", size, k << shift) for k in range(1, group)]
        current = pick(0)
        for block in received:
            current = current + block
    return current[0]


def all_gather_rows(part, size):
    row = lax.axis_index("row")
    current = part[None]
    for shift, group in reversed(row_stages(size)):
        me = (row >> shift) & (group - 1)
        received = [swap(current, "row", size, k << shift) for k in range(1, group)]
        whole = jnp.zeros((current.shape[0], group) + current.shape[1:], current.dtype)
        for k, block in enumerate([current] + received):
            whole = lax.dynamic_update_index_in_dim(whole, block, me ^ k, 1)
        current = whole.reshape((current.shape[0] * group,) + current.shape[1:])
    return current.reshape((-1, part.shape[1]))


def all_reduce_cols(part, size):
    received = [swap(part, "col", size, k) for k in range(1, size)]
    for block in received:
        part = part + block
    return part


def make_per_device(rows_size, cols_size):
    def per_device(vectors, panels, tfactors):
        col = lax.axis_index("col")
        local_rows, eigvecs = vectors.shape
        own = panels.shape[2]
        width = own * cols_size
        out_cols = eigvecs // cols_size

        vt = panels.transpose(0, 2, 1)
        pieces = []
        for k in range(cols_size):
            piece = lax.dynamic_slice_in_dim(vt, (col ^ k) * local_rows, local_rows, 2)
            pieces.append(swap(piece, "col", cols_size, k) if k else piece)
        house = jnp.zeros((2, cols_size, own, local_rows), jnp.float32)
        for k, piece in enumerate(pieces):
            house = lax.dynamic_update_index_in_dim(house, piece, col ^ k, 1)
        house = house.reshape((2, width, local_rows))

        u1 = matmul(tfactors[0], house[0], ((1,), (0,)))
        u2 = matmul(tfactors[1], house[1], ((1,), (0,)))
        scaled = matmul(jnp.concatenate([u1, u2], 0), vectors, ((1,), (0,)))
        cross = matmul(u2, house[0], ((1,), (1,)))
        half = width // 2
        cross = jnp.concatenate([cross[:, :half], cross[:, half:]], 0)
        partial = jnp.concatenate([scaled, cross], 1)

        part = reduce_scatter_rows(partial, rows_size)
        part = all_reduce_cols(part, cols_size)
        total = all_gather_rows(part, rows_size)

        scaled = total[:, :eigvecs]
        cross = jnp.concatenate([total[:width, eigvecs:], total[width:, eigvecs:]], 1)
        first = house[0] - matmul(cross, house[1], ((0,), (0,)))
        both = jnp.concatenate([first, house[1]], 0)
        result = vectors - matmul(both, scaled, ((0,), (0,)))

        out = jnp.zeros((cols_size, local_rows, out_cols), jnp.float32)
        for k in range(cols_size):
            block = lax.dynamic_slice_in_dim(result, (col ^ k) * out_cols, out_cols, 1)
            block = swap(block, "col", cols_size, k) if k else block
            out = lax.dynamic_update_index_in_dim(out, block, col ^ k, 0)
        return out.reshape((cols_size * local_rows, out_cols))

    return per_device


def solution(mesh):
    in_specs = (P(("row", "col"), None), P(None, "row", "col"), P())
    out_specs = P("row", "col")
    per_device = make_per_device(mesh.shape["row"], mesh.shape["col"])
    return jax.shard_map(
        per_device, mesh=mesh, in_specs=in_specs, out_specs=out_specs, check_vma=False
    )
```

```python
import functools

import jax
import jax.numpy as jnp
from jax import lax
from jax.experimental import pallas as pl
from jax.experimental.pallas import tpu as pltpu
from jax.sharding import PartitionSpec as P

PLAIN = ((1,), (0,))
BY_TRANSPOSE = ((1,), (1,))
FROM_TRANSPOSE = ((0,), (0,))


def split(value):
    high = value.astype(jnp.bfloat16)
    return high, (value - high.astype(jnp.float32)).astype(jnp.bfloat16)


def product(left, right, contract):
    def one(a, b):
        return lax.dot_general(a, b, (contract, ((), ())), preferred_element_type=jnp.float32)

    return one(left[0], right[0]) + (one(left[0], right[1]) + one(left[1], right[0]))


def kernel_call(body, shapes, *args, scratch=()):
    specs = [pl.BlockSpec(memory_space=pltpu.SMEM)]
    specs += [pl.BlockSpec(memory_space=pltpu.VMEM)] * (len(args) - 1)
    return pl.pallas_call(
        body,
        out_shape=[jax.ShapeDtypeStruct(shape, jnp.float32) for shape in shapes],
        in_specs=specs,
        out_specs=[pl.BlockSpec(memory_space=pltpu.VMEM)] * len(shapes),
        scratch_shapes=list(scratch),
        compiler_params=pltpu.CompilerParams(vmem_limit_bytes=32 * 1024 * 1024),
    )(*args)


def swap(block, axis, size, mask):
    return lax.ppermute(block, axis, [(i, i ^ mask) for i in range(size)])


def row_stages(size):
    stages = []
    shift = 0
    while (1 << shift) < size:
        bits = 1 if shift == 0 or (2 << shift) == size else 2
        stages.append((shift, 1 << bits))
        shift += bits
    return stages


def exchange_order(group):
    return [3, 1, 2] if group == 4 else list(range(1, group))


def cut_parts(parts, core, results, keep, send):
    rows = keep.shape[1]
    for j in range(parts // 2):
        at = 0
        for result in results:
            cut = pl.ds(at, result.shape[1])
            even = result[2 * j * rows : (2 * j + 1) * rows]
            odd = result[(2 * j + 1) * rows : (2 * j + 2) * rows]
            keep[j, :, cut] = jnp.where(core == 0, even, odd)
            send[j, :, cut] = jnp.where(core == 0, odd, even)
            at += result.shape[1]


def near_kernel(parts, *refs):
    place, pieces, field, keep, send, house = refs[0], refs[1:-4], refs[-4], refs[-3], refs[-2], refs[-1]
    col, core = place[0], place[1] & 1
    own, near = pieces[0].shape[1], len(pieces)
    for k, piece in enumerate(pieces):
        at = pl.multiple_of(((col ^ k) & (near - 1)) * own, own)
        house[pl.ds(at, own), :] = piece[0]
        house[pl.ds(near * own + at, own), :] = piece[1]
    result = product(split(house[...]), split(field[...]), PLAIN)
    cut_parts(parts, core, [result], keep, send)


def far_kernel(parts, *refs):
    place, pieces, field, keep, send, house, far = refs[0], refs[1:-5], refs[-5], refs[-4], refs[-3], refs[-2], refs[-1]
    col, core = place[0], place[1] & 1
    own, near = pieces[0].shape[1], len(pieces) // 2
    for k, piece in enumerate(pieces):
        at = pl.ds(pl.multiple_of((col ^ k) * own, own), own)
        house[0, at, :] = piece[0]
        house[1, at, :] = piece[1]
        if k >= near:
            at = pl.multiple_of(((col ^ k) & (near - 1)) * own, own)
            far[pl.ds(at, own), :] = piece[0]
            far[pl.ds(near * own + at, own), :] = piece[1]
    result = product(split(far[...]), split(field[...]), PLAIN)
    cross = product(split(house[1]), split(house[0]), BY_TRANSPOSE)
    cut_parts(parts, core, [result, cross], keep, send)


def merge_kernel(near, *refs):
    place, sources, same, out = refs[0], refs[1:-2], refs[-2], refs[-1]
    total = sources[0][0]
    for source in sources[1:]:
        total = total + source[0]
    eigvecs = same.shape[2]
    low = place[0] < near
    near_w, far_w = same[0], total[:, :eigvecs]
    out[0, :, :eigvecs] = jnp.where(low, near_w, far_w)
    out[0, :, eigvecs : 2 * eigvecs] = jnp.where(low, far_w, near_w)
    out[0, :, 2 * eigvecs :] = total[:, 2 * eigvecs - eigvecs :]


def add_split_kernel(shift, group, *refs):
    place, sources, outs = refs[0], refs[1:-group], refs[-group:]
    me = (place[1] >> shift) & (group - 1)
    for a in range(outs[0].shape[0]):
        for k, out in enumerate(outs):
            at = a * group + (me ^ k)
            total = sources[0][at]
            for source in sources[1:]:
                total = total + source[at]
            out[a] = total


def tail_kernel(cols_size, *refs):
    place, mine, other, factors, field, house = refs[:6]
    outs, scratch = refs[6:-1], refs[-1]
    col, core = place[0], place[1] & 1
    rows = mine.shape[1]
    for j in range(mine.shape[0]):
        a, b = mine[j], other[j]
        scratch[2 * j * rows : (2 * j + 1) * rows, :] = jnp.where(core == 0, a, b)
        scratch[(2 * j + 1) * rows : (2 * j + 2) * rows, :] = jnp.where(core == 0, b, a)
    eigvecs = field.shape[1]
    half = scratch.shape[0] // 2

    def weights(panel):
        rows = slice(panel * half, (panel + 1) * half)
        return jnp.concatenate([scratch[rows, :eigvecs], scratch[rows, eigvecs : 2 * eigvecs]], 0)

    first = product(split(factors[0]), split(weights(0)), PLAIN)
    first = split(first)
    cross = split(scratch[:, 2 * eigvecs :])
    second = weights(1) - product(cross, first, PLAIN)
    second = split(product(split(factors[1]), split(second), PLAIN))
    result = field[...] - (
        product(split(house[0]), first, FROM_TRANSPOSE)
        + product(split(house[1]), second, FROM_TRANSPOSE)
    )
    width = outs[0].shape[1]
    scratch_cols = [result[:, c * width : (c + 1) * width] for c in range(cols_size)]
    for c in range(cols_size):
        for k in range(cols_size):

            @pl.when(col == (c ^ k))
            def _(c=c, k=k):
                outs[k][...] = scratch_cols[c]


def all_reduce_cols(part, rows_size, cols_size):
    bits = cols_size.bit_length() - 1
    for step in range(bits):
        pairs = []
        for row in range(rows_size):
            mask = 1 << (bits - 1 - step if row & 1 else step)
            for col in range(cols_size):
                pairs.append((row * cols_size + col, row * cols_size + (col ^ mask)))
        part = part + lax.ppermute(part, ("row", "col"), pairs)
    return part


def make_per_device(rows_size, cols_size):
    stages = row_stages(rows_size)

    def per_device(vectors, panels, tfactors):
        col, row = lax.axis_index("col"), lax.axis_index("row")
        place = jnp.stack([col, row]).astype(jnp.int32)
        local_rows, eigvecs = vectors.shape
        own = panels.shape[2]
        width = own * cols_size
        out_cols = eigvecs // cols_size
        rows = width // rows_size
        wide = 2 * eigvecs + width

        vt = panels.transpose(0, 2, 1)
        pieces = [None] * cols_size
        for k in list(range(cols_size - 1, 0, -1)) + [0]:
            piece = lax.dynamic_slice_in_dim(vt, (col ^ k) * local_rows, local_rows, 2)
            pieces[k] = swap(piece, "col", cols_size, k) if k else piece

        near = cols_size // 2
        half = rows_size // 2

        def scatter(place, sources):
            for shift, group in stages[1:]:
                shape = (sources[0].shape[0] // group,) + sources[0].shape[1:]
                body = functools.partial(add_split_kernel, shift, group)
                cuts = kernel_call(body, [shape] * group, place, *sources)
                sources = [cuts[0]]
                for k in exchange_order(group):
                    sources.append(swap(cuts[k], "row", rows_size, k << shift))
            return sources

        def near_part(i, carry):
            at = place + i
            keep, send = kernel_call(
                functools.partial(near_kernel, rows_size),
                [(half, rows, eigvecs)] * 2,
                at,
                *pieces[:near],
                vectors,
                scratch=[pltpu.VMEM((width, local_rows), jnp.float32)],
            )
            first, *others = scatter(at, [keep, swap(send, "row", rows_size, 1)])
            for other in others:
                first = first + other
            return first

        same = lax.fori_loop(
            0, 1 + (row >> 10), near_part, jnp.zeros((1, rows, eigvecs), jnp.float32)
        )
        (pieces[near:], same) = lax.optimization_barrier((pieces[near:], same))
        keep, send, house = kernel_call(
            functools.partial(far_kernel, rows_size),
            [(half, rows, eigvecs + width)] * 2 + [(2, width, local_rows)],
            place,
            *pieces,
            vectors,
            scratch=[pltpu.VMEM((width, local_rows), jnp.float32)],
        )
        sources = scatter(place, [keep, swap(send, "row", rows_size, 1)])
        (part,) = kernel_call(
            functools.partial(merge_kernel, near), [(1, rows, wide)], place, *sources, same
        )
        current = all_reduce_cols(part, rows_size, cols_size)
        for shift, group in reversed(stages[1:]):
            me = (row >> shift) & (group - 1)
            whole = jnp.zeros((current.shape[0], group) + current.shape[1:], current.dtype)
            whole = lax.dynamic_update_index_in_dim(whole, current, me, 1)
            for k in exchange_order(group):
                block = swap(current, "row", rows_size, k << shift)
                whole = lax.dynamic_update_index_in_dim(whole, block, me ^ k, 1)
            current = whole.reshape((current.shape[0] * group,) + current.shape[1:])
        other = swap(current, "row", rows_size, 1)

        blocks = pl.pallas_call(
            functools.partial(tail_kernel, cols_size),
            out_shape=[jax.ShapeDtypeStruct((local_rows, out_cols), jnp.float32)] * cols_size,
            in_specs=[pl.BlockSpec(memory_space=pltpu.SMEM)]
            + [pl.BlockSpec(memory_space=pltpu.VMEM)] * 5,
            out_specs=[pl.BlockSpec(memory_space=pltpu.VMEM)] * cols_size,
            scratch_shapes=[pltpu.VMEM((width, wide), jnp.float32)],
            compiler_params=pltpu.CompilerParams(vmem_limit_bytes=32 * 1024 * 1024),
        )(place, current, other, tfactors, vectors, house)
        out = jnp.zeros((cols_size, local_rows, out_cols), jnp.float32)
        for k in list(range(1, cols_size)) + [0]:
            block = swap(blocks[k], "col", cols_size, k) if k else blocks[0]
            out = lax.dynamic_update_index_in_dim(out, block, col ^ k, 0)
        return out.reshape((cols_size * local_rows, out_cols))

    return per_device


def solution(mesh):
    in_specs = (P(("row", "col"), None), P(None, "row", "col"), P())
    out_specs = P("row", "col")
    per_device = make_per_device(mesh.shape["row"], mesh.shape["col"])
    return jax.shard_map(
        per_device, mesh=mesh, in_specs=in_specs, out_specs=out_specs, check_vma=False
    )
```

```python
import functools

import jax
import jax.numpy as jnp
from jax import lax
from jax.experimental import pallas as pl
from jax.experimental.pallas import tpu as pltpu
from jax.sharding import PartitionSpec as P

PLAIN = ((1,), (0,))
BY_TRANSPOSE = ((1,), (1,))
FROM_TRANSPOSE = ((0,), (0,))


def split(value):
    high = value.astype(jnp.bfloat16)
    return high, (value - high.astype(jnp.float32)).astype(jnp.bfloat16)


def product(left, right, contract=PLAIN):
    def one(a, b):
        return lax.dot_general(a, b, (contract, ((), ())), preferred_element_type=jnp.float32)

    return one(left[0], right[0]) + (one(left[0], right[1]) + one(left[1], right[0]))


def kernel_call(body, shapes, place, *args, scratch=()):
    specs = [pl.BlockSpec(memory_space=pltpu.SMEM)]
    specs += [pl.BlockSpec(memory_space=pltpu.VMEM)] * len(args)
    return pl.pallas_call(
        body,
        out_shape=[jax.ShapeDtypeStruct(shape, jnp.float32) for shape in shapes],
        in_specs=specs,
        out_specs=[pl.BlockSpec(memory_space=pltpu.VMEM)] * len(shapes),
        scratch_shapes=[pltpu.VMEM(shape, kind) for shape, kind in scratch],
        compiler_params=pltpu.CompilerParams(vmem_limit_bytes=24 * 1024 * 1024),
    )(place, *args)


def swap(block, axis, size, mask):
    return lax.ppermute(block, axis, [(i, i ^ mask) for i in range(size)])


def row_stages(size):
    stages = []
    shift = 0
    while (1 << shift) < size:
        bits = 1 if shift == 0 or (2 << shift) == size else 2
        stages.append((shift, 1 << bits))
        shift += bits
    return stages


def exchange_order(group):
    return [2, 1, 3] if group == 4 else list(range(1, group))


def join_kernel(steps, cols_size, *refs):
    place, blocks, out, sem = refs[0], refs[1 : 1 + len(steps)], refs[-2], refs[-1]
    copies = []
    for i, (step, block) in enumerate(zip(steps, blocks)):
        source = turn(place[0], -step, cols_size)
        copies.append(pltpu.make_async_copy(block, out.at[source], sem.at[i]))
    for copy in copies:
        copy.start()
    for copy in copies:
        copy.wait()


def turn(col, step, size):
    bits = size.bit_length() - 1

    def reverse(value):
        return sum(((value >> i) & 1) << (bits - 1 - i) for i in range(bits))

    return reverse((reverse(col) + step) & (size - 1))


def near_kernel(parts, groups, cols_size, *refs):
    place, pieces, (field, keep, send, high, low) = refs[0], refs[1:-5], refs[-5:]
    col, core = place[0], place[1] & 1
    own, near = pieces[0].shape[1], len(pieces)
    for i, piece in enumerate(pieces):
        at = pl.multiple_of((turn(col, -i * groups, cols_size) & (near - 1)) * own, own)
        for panel in range(2):
            rows = pl.ds(panel * near * own + at, own)
            high[rows, :], low[rows, :] = split(piece[panel])
    result = product((high[...], low[...]), split(field[...]))
    for j in range(parts // 2):
        rows = keep.shape[1]
        even = result[2 * j * rows : (2 * j + 1) * rows]
        odd = result[(2 * j + 1) * rows : (2 * j + 2) * rows]
        keep[j] = jnp.where(core == 0, even, odd)
        send[j] = jnp.where(core == 0, odd, even)


def far_kernel(parts, steps, groups, *refs):
    place, pieces = refs[0], refs[1:-8]
    field, keep, send, house, high, low, far_h, far_l = refs[-8:]
    col, core = place[0], place[1] & 1
    cols_size = len(pieces)
    own, near = pieces[0].shape[1], cols_size // groups
    mine = col // near
    for step, piece in zip(steps, pieces):
        block = turn(col, -step, cols_size)
        group = block // near
        at = pl.multiple_of(block * own, own)
        slot = group - jnp.where(group > mine, 1, 0)
        inside = pl.multiple_of((slot * 2 * near + (block & (near - 1))) * own, own)
        for panel in range(2):
            value = piece[panel]
            rows = pl.ds(at, own)
            house[panel, rows, :] = value
            value_h, value_l = split(value)
            high[panel, rows, :], low[panel, rows, :] = value_h, value_l
            if step % groups:
                rows = pl.ds(inside + panel * near * own, own)
                far_h[rows, :], far_l[rows, :] = value_h, value_l
    result = product((far_h[...], far_l[...]), split(field[...]))
    cross = product((high[1], low[1]), (high[0], low[0]), BY_TRANSPOSE)
    height = 2 * near * own
    count = height // parts
    rows = cross.shape[0] // parts
    side = keep.shape[2] // cross.shape[1]
    packed = -(-rows // side)
    for j in range(parts // 2):
        for out, odd in ((keep, core), (send, 1 - core)):

            def chosen(value, first, number, stride):
                even = value[first : first + number]
                return jnp.where(odd == 0, even, value[first + stride : first + stride + number])

            for slot in range(groups - 1):
                at = slot * count
                block = chosen(result, slot * height + 2 * j * count, count, count)
                out[j, at : at + count, :] = block
            at = (groups - 1) * count
            if packed * side != rows:
                out[j, at:, :] = jnp.zeros((packed, keep.shape[2]), jnp.float32)
            for i in range(rows // packed):
                block = chosen(cross, 2 * j * rows + i * packed, packed, rows)
                out[j, at:, i * cross.shape[1] : (i + 1) * cross.shape[1]] = block


def add_split_kernel(shift, group, *refs):
    place, sources, outs = refs[0], refs[1:-group], refs[-group:]
    me = (place[1] >> shift) & (group - 1)
    for a in range(outs[0].shape[0]):
        for k, out in enumerate(outs):
            at = a * group + (me ^ k)
            total = sources[0][at]
            for source in sources[1:]:
                total = total + source[at]
            out[a] = total


def assemble_kernel(shift, group, *refs):
    place, blocks, out = refs[0], refs[1:-1], refs[-1]
    me = (place[1] >> shift) & (group - 1)
    for k, block in enumerate(blocks):
        for a in range(block.shape[0]):
            out[a * group + (me ^ k)] = block[a]


def tail_kernel(cols_size, groups, shift, ks, *refs):
    group = len(ks)
    place, blocks = refs[0], refs[1 : 1 + 2 * group]
    factors, house, field = refs[1 + 2 * group : 4 + 2 * group]
    outs, weights, cross = refs[4 + 2 * group : -2], refs[-2], refs[-1]
    col, core = place[0], place[1] & 1
    me = (place[1] >> shift) & (group - 1)
    width = house.shape[1]
    parts = 2 * group * blocks[0].shape[0]
    height = 2 * width // groups
    count = height // parts
    rows = width // parts
    packed = blocks[0].shape[1] - groups * count
    for i, block in enumerate(blocks):
        for a in range(block.shape[0]):
            p = 2 * (a * group + (me ^ ks[i % group])) + (core if i < group else 1 - core)
            start = p * count
            panel = start // (height // 2)
            start = panel * width + start - panel * (height // 2)
            for j in range(groups):
                at = pl.multiple_of(start + j * (height // 2), count)
                weights[pl.ds(at, count), :] = block[a, j * count : (j + 1) * count]
            for j in range(rows // packed):
                at = pl.multiple_of(p * rows + j * packed, packed)
                cut = slice(j * width, (j + 1) * width)
                cross[pl.ds(at, packed), :] = block[a, groups * count :, cut]

    first = split(product(split(factors[0]), split(weights[:width])))
    second = weights[width:] - product(split(cross[...]), first)
    second = split(product(split(factors[1]), split(second)))
    update = product(split(house[0]), first, FROM_TRANSPOSE)
    update = update + product(split(house[1]), second, FROM_TRANSPOSE)
    cols = outs[0].shape[1]
    result = field[...] - update
    for c in range(cols_size):
        for step, out in enumerate(outs):

            @pl.when(turn(col, step, cols_size) == c)
            def _(c=c, out=out):
                out[...] = result[:, c * cols : (c + 1) * cols]


def all_reduce_cols(part, rows_size, cols_size):
    bits = cols_size.bit_length() - 1
    for step in range(bits):
        pairs = []
        for row in range(rows_size):
            mask = 1 << (bits - 1 - step if row & 1 else step)
            for col in range(cols_size):
                pairs.append((row * cols_size + col, row * cols_size + (col ^ mask)))
        other = lax.ppermute(part, ("row", "col"), pairs)
        if step == bits - 1:
            return part, other
        part = part + other


def make_per_device(rows_size, cols_size):
    stages = row_stages(rows_size)
    bf16 = jnp.bfloat16

    def scatter(place, sources, stages):
        for shift, group in stages[1:]:
            shape = (sources[0].shape[0] // group,) + sources[0].shape[1:]
            body = functools.partial(add_split_kernel, shift, group)
            cuts = kernel_call(body, [shape] * group, place, *sources)
            sources = [cuts[0]]
            for k in exchange_order(group):
                sources.append(swap(cuts[k], "row", rows_size, k << shift))
        return functools.reduce(jnp.add, sources)

    def gather(place, current):
        for shift, group in reversed(stages[2:]):
            blocks = [current] * group
            for k in exchange_order(group):
                blocks[k] = swap(current, "row", rows_size, k << shift)
            body = functools.partial(assemble_kernel, shift, group)
            shape = (current.shape[0] * group,) + current.shape[1:]
            (current,) = kernel_call(body, [shape], place, *blocks)
        shift, group = stages[1]
        blocks = [current]
        for k in exchange_order(group):
            blocks.append(swap(current, "row", rows_size, k << shift))
        return blocks + [swap(block, "row", rows_size, 1) for block in blocks]

    def per_device(vectors, panels, tfactors):
        col, row = lax.axis_index("col"), lax.axis_index("row")
        place = jnp.stack([col, row]).astype(jnp.int32)
        always = (row >> 16) == 0
        local_rows, eigvecs = vectors.shape
        own = panels.shape[2]
        width = own * cols_size
        out_cols = eigvecs // cols_size
        half = rows_size // 2
        near = max(1, rows_size // (2 * own))
        groups = cols_size // near
        count = 2 * near * own // rows_size
        packed = -(-(width // rows_size) * width // eigvecs)

        vt = panels.transpose(0, 2, 1)
        pieces = [None] * cols_size
        steps = list(range(cols_size - 1, 0, -1))
        for batch in (steps[:1], steps[1:] + [0]):
            for k in batch:
                at = turn(col, k, cols_size) * local_rows
                pieces[k] = lax.dynamic_slice_in_dim(vt, at, local_rows, 2)
            cuts, vt = lax.optimization_barrier(([pieces[k] for k in batch], vt))
            for k, cut in zip(batch, cuts):
                pairs = [(i, turn(i, k, cols_size)) for i in range(cols_size)]
                pieces[k] = lax.ppermute(cut, "col", pairs) if k else cut

        def near_part():
            keep, send = kernel_call(
                functools.partial(near_kernel, rows_size, groups, cols_size),
                [(half, count, eigvecs)] * 2,
                place,
                *pieces[::groups],
                vectors,
                scratch=[((2 * near * own, local_rows), bf16)] * 2,
            )
            bits = [(i, 2) for i in range(rows_size.bit_length() - 1)]
            return scatter(place, [keep, swap(send, "row", rows_size, 1)], bits)

        same = lax.cond(
            always, near_part, lambda: jnp.zeros((1, count, eigvecs), jnp.float32)
        )
        steps = steps + [0]
        cuts, same = lax.optimization_barrier(([pieces[k] for k in steps], same))
        keep, send, house = kernel_call(
            functools.partial(far_kernel, rows_size, steps, groups),
            [(half, (groups - 1) * count + packed, eigvecs)] * 2 + [(2, width, local_rows)],
            place,
            *cuts,
            vectors,
            scratch=[((2, width, local_rows), bf16)] * 2
            + [((2 * (cols_size - near) * own, local_rows), bf16)] * 2,
        )
        rest = scatter(place, [keep, swap(send, "row", rows_size, 1)], stages)
        blocks = [rest[:, i * count : (i + 1) * count] for i in range(groups - 1)]
        mine = col // near
        part = []
        for group in range(groups):
            block = blocks[max(group - 1, 0)]
            if 0 < group < groups - 1:
                block = jnp.where(mine < group, block, blocks[group])
            part.append(jnp.where(mine == group, same, block))
        part = jnp.concatenate(part + [rest[:, (groups - 1) * count :]], 1)
        part, other = all_reduce_cols(part, rows_size, cols_size)

        blocks = kernel_call(
            functools.partial(
                tail_kernel, cols_size, groups, stages[1][0], [0] + exchange_order(stages[1][1])
            ),
            [(local_rows, out_cols)] * cols_size,
            place,
            *gather(place, part + other),
            tfactors,
            house,
            vectors,
            scratch=[((2 * width, eigvecs), jnp.float32), ((width, width), jnp.float32)],
        )
        blocks = list(blocks)
        for k in [3, 1, 2]:
            pairs = [(i, turn(i, k, cols_size)) for i in range(cols_size)]
            blocks[k] = lax.ppermute(blocks[k], "col", pairs)
        steps = [0, *range(cols_size - 1, 0, -2), *range(2, cols_size, 2)]
        out = pl.pallas_call(
            functools.partial(join_kernel, steps, cols_size),
            out_shape=jax.ShapeDtypeStruct((cols_size, local_rows, out_cols), jnp.float32),
            in_specs=[pl.BlockSpec(memory_space=pltpu.SMEM)]
            + [pl.BlockSpec(memory_space=pltpu.VMEM)] * cols_size,
            out_specs=pl.BlockSpec(memory_space=pl.ANY),
            scratch_shapes=[pltpu.SemaphoreType.DMA((cols_size,))],
            compiler_params=pltpu.CompilerParams(vmem_limit_bytes=4 * 1024 * 1024),
        )(place, *[blocks[k] for k in steps])
        return out.reshape((cols_size * local_rows, out_cols))

    return per_device


def solution(mesh):
    in_specs = (P(("row", "col"), None), P(None, "row", "col"), P())
    out_specs = P("row", "col")
    per_device = make_per_device(mesh.shape["row"], mesh.shape["col"])
    return jax.shard_map(
        per_device, mesh=mesh, in_specs=in_specs, out_specs=out_specs, check_vma=False
    )
```

```python
import functools

import jax
import jax.numpy as jnp
from jax import lax
from jax.experimental import pallas as pl
from jax.experimental.pallas import tpu as pltpu
from jax.sharding import PartitionSpec as P

PLAIN = ((1,), (0,))
BY_TRANSPOSE = ((1,), (1,))
FROM_TRANSPOSE = ((0,), (0,))


def split(value):
    high = value.astype(jnp.bfloat16)
    return high, (value - high.astype(jnp.float32)).astype(jnp.bfloat16)


def product(left, right, contract=PLAIN):
    def one(a, b):
        return lax.dot_general(a, b, (contract, ((), ())), preferred_element_type=jnp.float32)

    return one(left[0], right[0]) + (one(left[0], right[1]) + one(left[1], right[0]))


def here():
    return lax.axis_index("col"), lax.axis_index("row")


def kernel_call(body, shapes, *args, scratch=()):
    return pl.pallas_call(
        body,
        out_shape=[jax.ShapeDtypeStruct(shape, jnp.float32) for shape in shapes],
        in_specs=[pl.BlockSpec(memory_space=pltpu.VMEM)] * len(args),
        out_specs=[pl.BlockSpec(memory_space=pltpu.VMEM)] * len(shapes),
        scratch_shapes=[pltpu.VMEM(shape, kind) for shape, kind in scratch],
        compiler_params=pltpu.CompilerParams(vmem_limit_bytes=24 * 1024 * 1024),
    )(*args)


def swap(block, axis, size, mask):
    return lax.ppermute(block, axis, [(i, i ^ mask) for i in range(size)])


def row_stages(size):
    stages = []
    shift = 0
    while (1 << shift) < size:
        bits = 1 if shift == 0 or (2 << shift) == size else 2
        stages.append((shift, 1 << bits))
        shift += bits
    return stages


def exchange_order(group):
    return [2, 1, 3] if group == 4 else list(range(1, group))


def join_kernel(steps, cols_size, *refs):
    place, blocks, out, sem = here(), refs[: len(steps)], refs[-2], refs[-1]
    copies = []
    for i, (step, block) in enumerate(zip(steps, blocks)):
        source = turn(place[0], -step, cols_size)
        copies.append(pltpu.make_async_copy(block, out.at[source], sem.at[i]))
    for copy in copies:
        copy.start()
    for copy in copies:
        copy.wait()


def turn(col, step, size):
    bits = size.bit_length() - 1

    def reverse(value):
        return sum(((value >> i) & 1) << (bits - 1 - i) for i in range(bits))

    return reverse((reverse(col) + step) & (size - 1))


def near_kernel(parts, groups, cols_size, *refs):
    place, pieces, (field, keep, send, high, low) = here(), refs[:-5], refs[-5:]
    col, core = place[0], place[1] & 1
    own, near = pieces[0].shape[1], len(pieces)
    for i, piece in enumerate(pieces):
        at = pl.multiple_of((turn(col, -i * groups, cols_size) & (near - 1)) * own, own)
        for panel in range(2):
            rows = pl.ds(panel * near * own + at, own)
            high[rows, :], low[rows, :] = split(piece[panel])
    result = product((high[...], low[...]), split(field[...]))
    for j in range(parts // 2):
        rows = keep.shape[1]
        even = result[2 * j * rows : (2 * j + 1) * rows]
        odd = result[(2 * j + 1) * rows : (2 * j + 2) * rows]
        keep[j] = jnp.where(core == 0, even, odd)
        send[j] = jnp.where(core == 0, odd, even)


def far_kernel(parts, steps, groups, *refs):
    place, pieces = here(), refs[:-8]
    field, keep, send, house, high, low, far_h, far_l = refs[-8:]
    col, core = place[0], place[1] & 1
    cols_size = len(pieces)
    own, near = pieces[0].shape[1], cols_size // groups
    mine = col // near
    for step, piece in zip(steps, pieces):
        block = turn(col, -step, cols_size)
        group = block // near
        at = pl.multiple_of(block * own, own)
        slot = group - jnp.where(group > mine, 1, 0)
        inside = pl.multiple_of((slot * 2 * near + (block & (near - 1))) * own, own)
        for panel in range(2):
            value = piece[panel]
            rows = pl.ds(at, own)
            house[panel, rows, :] = value
            value_h, value_l = split(value)
            high[panel, rows, :], low[panel, rows, :] = value_h, value_l
            if step % groups:
                rows = pl.ds(inside + panel * near * own, own)
                far_h[rows, :], far_l[rows, :] = value_h, value_l
    result = product((far_h[...], far_l[...]), split(field[...]))
    cross = product((high[1], low[1]), (high[0], low[0]), BY_TRANSPOSE)
    height = 2 * near * own
    count = height // parts
    rows = cross.shape[0] // parts
    side = keep.shape[2] // cross.shape[1]
    packed = -(-rows // side)
    for j in range(parts // 2):
        for out, odd in ((keep, core), (send, 1 - core)):

            def chosen(value, first, number, stride):
                even = value[first : first + number]
                return jnp.where(odd == 0, even, value[first + stride : first + stride + number])

            for slot in range(groups - 1):
                at = slot * count
                block = chosen(result, slot * height + 2 * j * count, count, count)
                out[j, at : at + count, :] = block
            at = (groups - 1) * count
            if packed * side != rows:
                out[j, at:, :] = jnp.zeros((packed, keep.shape[2]), jnp.float32)
            for i in range(rows // packed):
                block = chosen(cross, 2 * j * rows + i * packed, packed, rows)
                out[j, at:, i * cross.shape[1] : (i + 1) * cross.shape[1]] = block


def add_split_kernel(shift, group, *refs):
    place, sources, outs = here(), refs[:-group], refs[-group:]
    me = (place[1] >> shift) & (group - 1)
    for a in range(outs[0].shape[0]):
        for k, out in enumerate(outs):
            at = a * group + (me ^ k)
            total = sources[0][at]
            for source in sources[1:]:
                total = total + source[at]
            out[a] = total


def assemble_kernel(shift, group, *refs):
    place, blocks, out = here(), refs[:-1], refs[-1]
    me = (place[1] >> shift) & (group - 1)
    for k, block in enumerate(blocks):
        for a in range(block.shape[0]):
            out[a * group + (me ^ k)] = block[a]


def tail_kernel(cols_size, groups, shift, ks, *refs):
    group = len(ks)
    place, blocks = here(), refs[: 2 * group]
    factors, house, field = refs[2 * group : 3 + 2 * group]
    outs, weights, cross = refs[3 + 2 * group : -2], refs[-2], refs[-1]
    col, core = place[0], place[1] & 1
    me = (place[1] >> shift) & (group - 1)
    width = house.shape[1]
    parts = 2 * group * blocks[0].shape[0]
    height = 2 * width // groups
    count = height // parts
    rows = width // parts
    packed = blocks[0].shape[1] - groups * count
    for i, block in enumerate(blocks):
        for a in range(block.shape[0]):
            p = 2 * (a * group + (me ^ ks[i % group])) + (core if i < group else 1 - core)
            start = p * count
            panel = start // (height // 2)
            start = panel * width + start - panel * (height // 2)
            for j in range(groups):
                at = pl.multiple_of(start + j * (height // 2), count)
                weights[pl.ds(at, count), :] = block[a, j * count : (j + 1) * count]
            for j in range(rows // packed):
                at = pl.multiple_of(p * rows + j * packed, packed)
                cut = slice(j * width, (j + 1) * width)
                cross[pl.ds(at, packed), :] = block[a, groups * count :, cut]

    first = split(product(split(factors[0]), split(weights[:width])))
    second = weights[width:] - product(split(cross[...]), first)
    second = split(product(split(factors[1]), split(second)))
    update = product(split(house[0]), first, FROM_TRANSPOSE)
    update = update + product(split(house[1]), second, FROM_TRANSPOSE)
    cols = outs[0].shape[1]
    result = field[...] - update
    for c in range(cols_size):
        for step, out in enumerate(outs):

            @pl.when(turn(col, step, cols_size) == c)
            def _(c=c, out=out):
                out[...] = result[:, c * cols : (c + 1) * cols]


def all_reduce_cols(part, rows_size, cols_size):
    bits = cols_size.bit_length() - 1
    for step in range(bits):
        pairs = []
        for row in range(rows_size):
            mask = 1 << (bits - 1 - step if row & 1 else step)
            for col in range(cols_size):
                pairs.append((row * cols_size + col, row * cols_size + (col ^ mask)))
        other = lax.ppermute(part, ("row", "col"), pairs)
        if step == bits - 1:
            return part, other
        part = part + other


def make_per_device(rows_size, cols_size):
    stages = row_stages(rows_size)
    bf16 = jnp.bfloat16

    def scatter(sources, stages):
        for shift, group in stages[1:]:
            shape = (sources[0].shape[0] // group,) + sources[0].shape[1:]
            body = functools.partial(add_split_kernel, shift, group)
            cuts = kernel_call(body, [shape] * group, *sources)
            sources = [cuts[0]]
            for k in exchange_order(group):
                sources.append(swap(cuts[k], "row", rows_size, k << shift))
        return functools.reduce(jnp.add, sources)

    def gather(current):
        for shift, group in reversed(stages[2:]):
            blocks = [current] * group
            for k in exchange_order(group):
                blocks[k] = swap(current, "row", rows_size, k << shift)
            body = functools.partial(assemble_kernel, shift, group)
            shape = (current.shape[0] * group,) + current.shape[1:]
            (current,) = kernel_call(body, [shape], *blocks)
        shift, group = stages[1]
        blocks = [current]
        for k in exchange_order(group):
            blocks.append(swap(current, "row", rows_size, k << shift))
        return blocks + [swap(block, "row", rows_size, 1) for block in blocks]

    def per_device(vectors, panels, tfactors):
        col, row = lax.axis_index("col"), lax.axis_index("row")
        always = (row >> 16) == 0
        local_rows, eigvecs = vectors.shape
        own = panels.shape[2]
        width = own * cols_size
        out_cols = eigvecs // cols_size
        half = rows_size // 2
        near = max(1, rows_size // (2 * own))
        groups = cols_size // near
        count = 2 * near * own // rows_size
        packed = -(-(width // rows_size) * width // eigvecs)

        vt = panels.transpose(0, 2, 1)
        pieces = [None] * cols_size
        steps = list(range(cols_size - 1, 0, -1))
        for batch in (steps[:1], steps[1:] + [0]):
            for k in batch:
                at = turn(col, k, cols_size) * local_rows
                pieces[k] = lax.dynamic_slice_in_dim(vt, at, local_rows, 2)
            cuts, vt = lax.optimization_barrier(([pieces[k] for k in batch], vt))
            for k, cut in zip(batch, cuts):
                pairs = [(i, turn(i, k, cols_size)) for i in range(cols_size)]
                pieces[k] = lax.ppermute(cut, "col", pairs) if k else cut

        def near_part():
            keep, send = kernel_call(
                functools.partial(near_kernel, rows_size, groups, cols_size),
                [(half, count, eigvecs)] * 2,
                *pieces[::groups],
                vectors,
                scratch=[((2 * near * own, local_rows), bf16)] * 2,
            )
            bits = [(i, 2) for i in range(rows_size.bit_length() - 1)]
            return scatter([keep, swap(send, "row", rows_size, 1)], bits)

        same = lax.cond(
            always, near_part, lambda: jnp.zeros((1, count, eigvecs), jnp.float32)
        )
        steps = steps + [0]
        cuts, same = lax.optimization_barrier(([pieces[k] for k in steps], same))
        keep, send, house = kernel_call(
            functools.partial(far_kernel, rows_size, steps, groups),
            [(half, (groups - 1) * count + packed, eigvecs)] * 2 + [(2, width, local_rows)],
            *cuts,
            vectors,
            scratch=[((2, width, local_rows), bf16)] * 2
            + [((2 * (cols_size - near) * own, local_rows), bf16)] * 2,
        )
        rest = scatter([keep, swap(send, "row", rows_size, 1)], stages)
        blocks = [rest[:, i * count : (i + 1) * count] for i in range(groups - 1)]
        mine = col // near
        part = []
        for group in range(groups):
            block = blocks[max(group - 1, 0)]
            if 0 < group < groups - 1:
                block = jnp.where(mine < group, block, blocks[group])
            part.append(jnp.where(mine == group, same, block))
        part = jnp.concatenate(part + [rest[:, (groups - 1) * count :]], 1)
        part, other = all_reduce_cols(part, rows_size, cols_size)

        blocks = kernel_call(
            functools.partial(
                tail_kernel, cols_size, groups, stages[1][0], [0] + exchange_order(stages[1][1])
            ),
            [(local_rows, out_cols)] * cols_size,
            *gather(part + other),
            tfactors,
            house,
            vectors,
            scratch=[((2 * width, eigvecs), jnp.float32), ((width, width), jnp.float32)],
        )
        blocks = list(blocks)
        for k in [3, 1, 2]:
            pairs = [(i, turn(i, k, cols_size)) for i in range(cols_size)]
            blocks[k] = lax.ppermute(blocks[k], "col", pairs)
        steps = [0, *range(cols_size - 1, 0, -2), *range(2, cols_size, 2)]
        out = pl.pallas_call(
            functools.partial(join_kernel, steps, cols_size),
            out_shape=jax.ShapeDtypeStruct((cols_size, local_rows, out_cols), jnp.float32),
            in_specs=[pl.BlockSpec(memory_space=pltpu.VMEM)] * cols_size,
            out_specs=pl.BlockSpec(memory_space=pl.ANY),
            scratch_shapes=[pltpu.SemaphoreType.DMA((cols_size,))],
            compiler_params=pltpu.CompilerParams(vmem_limit_bytes=4 * 1024 * 1024),
        )(*[blocks[k] for k in steps])
        return out.reshape((cols_size * local_rows, out_cols))

    return per_device


def solution(mesh):
    in_specs = (P(("row", "col"), None), P(None, "row", "col"), P())
    out_specs = P("row", "col")
    per_device = make_per_device(mesh.shape["row"], mesh.shape["col"])
    return jax.shard_map(
        per_device, mesh=mesh, in_specs=in_specs, out_specs=out_specs, check_vma=False
    )
```

```python
import functools

import jax
import jax.numpy as jnp
from jax import lax
from jax.experimental import pallas as pl
from jax.experimental.pallas import tpu as pltpu
from jax.sharding import PartitionSpec as P

PLAIN = ((1,), (0,))
BY_TRANSPOSE = ((1,), (1,))
FROM_TRANSPOSE = ((0,), (0,))


def split(value):
    high = value.astype(jnp.bfloat16)
    return high, (value - high.astype(jnp.float32)).astype(jnp.bfloat16)


def product(left, right, contract=PLAIN):
    def one(a, b):
        return lax.dot_general(a, b, (contract, ((), ())), preferred_element_type=jnp.float32)

    return one(left[0], right[0]) + (one(left[0], right[1]) + one(left[1], right[0]))


def here():
    return lax.axis_index("col"), lax.axis_index("row")


def kernel_call(body, shapes, *args, scratch=()):
    return pl.pallas_call(
        body,
        out_shape=[jax.ShapeDtypeStruct(shape, jnp.float32) for shape in shapes],
        in_specs=[pl.BlockSpec(memory_space=pltpu.VMEM)] * len(args),
        out_specs=[pl.BlockSpec(memory_space=pltpu.VMEM)] * len(shapes),
        scratch_shapes=[pltpu.VMEM(shape, kind) for shape, kind in scratch],
        compiler_params=pltpu.CompilerParams(vmem_limit_bytes=24 * 1024 * 1024),
    )(*args)


def swap(block, axis, size, mask):
    return lax.ppermute(block, axis, [(i, i ^ mask) for i in range(size)])


def row_stages(size):
    stages = []
    shift = 0
    while (1 << shift) < size:
        bits = 1 if shift == 0 or (2 << shift) == size else 2
        stages.append((shift, 1 << bits))
        shift += bits
    return stages


def exchange_order(group):
    return [2, 1, 3] if group == 4 else list(range(1, group))


def join_kernel(steps, cols_size, *refs):
    place, blocks, out, sem = here(), refs[: len(steps)], refs[-2], refs[-1]
    copies = []
    for i, (step, block) in enumerate(zip(steps, blocks)):
        source = turn(place[0], -step, cols_size)
        copies.append(pltpu.make_async_copy(block, out.at[source], sem.at[i]))
    for copy in copies:
        copy.start()
    for copy in copies:
        copy.wait()


def reverse(value, size):
    bits = size.bit_length() - 1
    return sum(((value >> i) & 1) << (bits - 1 - i) for i in range(bits))


def turn(col, step, size):
    return reverse((reverse(col, size) + step) & (size - 1), size)


def near_kernel(parts, steps, cols_size, *refs):
    place, pieces, (field, keep, send, high, low) = here(), refs[:-5], refs[-5:]
    col, core = place[0], place[1] & 1
    own, near = pieces[0].shape[1], len(pieces)
    for step, piece in zip(steps, pieces):
        at = pl.multiple_of((turn(col, -step, cols_size) & (near - 1)) * own, own)
        for panel in range(2):
            rows = pl.ds(panel * near * own + at, own)
            high[rows, :], low[rows, :] = split(piece[panel])
    result = product((high[...], low[...]), split(field[...]))
    for j in range(parts // 2):
        rows = keep.shape[1]
        even = result[2 * j * rows : (2 * j + 1) * rows]
        odd = result[(2 * j + 1) * rows : (2 * j + 2) * rows]
        keep[j] = jnp.where(core == 0, even, odd)
        send[j] = jnp.where(core == 0, odd, even)


def far_kernel(parts, steps, groups, rest, last, cols_size, *refs):
    place, pieces, refs = here(), refs[: len(steps)], refs[len(steps) :]
    if last:
        field, keep, send, house, high, low, far_h, far_l = refs
    else:
        field, keep, send, far_h, far_l = refs
    col, core = place[0], place[1] & 1
    own, near = pieces[0].shape[1], cols_size // groups
    for step, piece in zip(steps, pieces):
        block = turn(col, -step, cols_size)
        at = pl.multiple_of(block * own, own)
        inside = pl.multiple_of((block & (near - 1)) * own, own)
        for panel in range(2):
            value = piece[panel]
            rows = pl.ds(at, own)
            value_h, value_l = split(value)
            if last:
                house[panel, rows, :] = value
                high[panel, rows, :], low[panel, rows, :] = value_h, value_l
            if step % groups in rest:
                slot = 2 * rest.index(step % groups) + panel
                rows = pl.ds(inside + slot * near * own, own)
                far_h[rows, :], far_l[rows, :] = value_h, value_l
    if rest:
        result = product((far_h[...], far_l[...]), split(field[...]))
    height = 2 * near * own
    count = height // parts
    if last:
        cross = product((high[1], low[1]), (high[0], low[0]), BY_TRANSPOSE)
        rows = cross.shape[0] // parts
        side = keep.shape[2] // cross.shape[1]
        packed = -(-rows // side)
    for j in range(parts // 2):
        for out, odd in ((keep, core), (send, 1 - core)):

            def chosen(value, first, number, stride):
                even = value[first : first + number]
                return jnp.where(odd == 0, even, value[first + stride : first + stride + number])

            for slot in range(len(rest)):
                at = slot * count
                block = chosen(result, slot * height + 2 * j * count, count, count)
                out[j, at : at + count, :] = block
            if not last:
                continue
            at = len(rest) * count
            if packed * side != rows:
                out[j, at:, :] = jnp.zeros((packed, keep.shape[2]), jnp.float32)
            for i in range(rows // packed):
                block = chosen(cross, 2 * j * rows + i * packed, packed, rows)
                out[j, at:, i * cross.shape[1] : (i + 1) * cross.shape[1]] = block


def add_split_kernel(shift, group, terms, *refs):
    place, sources, outs = here(), refs[:-group], refs[-group:]
    me = (place[1] >> shift) & (group - 1)
    first = 0
    for i in range(0, len(sources), terms):
        rows = slice(first, first + sources[i].shape[1])
        first += sources[i].shape[1]
        for a in range(outs[0].shape[0]):
            for k, out in enumerate(outs):
                at = a * group + (me ^ k)
                total = sources[i][at]
                for source in sources[i + 1 : i + terms]:
                    total = total + source[at]
                out[a, rows] = total


def merge_kernel(cols_size, groups, order, *refs):
    place, early, sources = here(), refs[: groups - len(order)], refs[groups - len(order) : -2]
    out, scratch = refs[-2:]
    count = early[0].shape[1]
    total = sources[0][0]
    for source in sources[1:]:
        total = total + source[0]
    for distance, block in zip([d for d in range(groups) if d not in order], early):
        scratch[distance] = block[0]
    for i, distance in enumerate(order):
        scratch[distance] = total[i * count : (i + 1) * count]
    mine = reverse(place[0] // (cols_size // groups), groups)
    for group in range(groups):
        distance = (mine - reverse(group, groups)) & (groups - 1)
        out[0, group * count : (group + 1) * count] = scratch[distance]
    out[0, groups * count :] = total[len(order) * count :]


def assemble_kernel(shift, group, *refs):
    place, blocks, out = here(), refs[:-1], refs[-1]
    me = (place[1] >> shift) & (group - 1)
    for k, block in enumerate(blocks):
        for a in range(block.shape[0]):
            out[a * group + (me ^ k)] = block[a]


def tail_kernel(cols_size, groups, shift, ks, *refs):
    group = len(ks)
    place, blocks = here(), refs[: 2 * group]
    factors, house, field = refs[2 * group : 3 + 2 * group]
    outs, weights, cross = refs[3 + 2 * group : -2], refs[-2], refs[-1]
    col, core = place[0], place[1] & 1
    me = (place[1] >> shift) & (group - 1)
    width = house.shape[1]
    parts = 2 * group * blocks[0].shape[0]
    height = 2 * width // groups
    count = height // parts
    rows = width // parts
    packed = blocks[0].shape[1] - groups * count
    for i, block in enumerate(blocks):
        for a in range(block.shape[0]):
            p = 2 * (a * group + (me ^ ks[i % group])) + (core if i < group else 1 - core)
            start = p * count
            panel = start // (height // 2)
            start = panel * width + start - panel * (height // 2)
            for j in range(groups):
                at = pl.multiple_of(start + j * (height // 2), count)
                weights[pl.ds(at, count), :] = block[a, j * count : (j + 1) * count]
            for j in range(rows // packed):
                at = pl.multiple_of(p * rows + j * packed, packed)
                cut = slice(j * width, (j + 1) * width)
                cross[pl.ds(at, packed), :] = block[a, groups * count :, cut]

    first = split(product(split(factors[0]), split(weights[:width])))
    second = weights[width:] - product(split(cross[...]), first)
    second = split(product(split(factors[1]), split(second)))
    update = product(split(house[0]), first, FROM_TRANSPOSE)
    update = update + product(split(house[1]), second, FROM_TRANSPOSE)
    cols = outs[0].shape[1]
    result = field[...] - update
    for c in range(cols_size):
        for step, out in enumerate(outs):

            @pl.when(turn(col, step, cols_size) == c)
            def _(c=c, out=out):
                out[...] = result[:, c * cols : (c + 1) * cols]


def all_reduce_cols(part, rows_size, cols_size):
    bits = cols_size.bit_length() - 1
    for step in range(bits):
        pairs = []
        for row in range(rows_size):
            mask = 1 << (bits - 1 - step if row & 1 else step)
            for col in range(cols_size):
                pairs.append((row * cols_size + col, row * cols_size + (col ^ mask)))
        other = lax.ppermute(part, ("row", "col"), pairs)
        if step == bits - 1:
            return part, other
        part = part + other


def make_per_device(rows_size, cols_size):
    stages = row_stages(rows_size)
    bf16 = jnp.bfloat16

    def exchanged(sources, stages):
        terms = 2
        for shift, group in stages[1:]:
            rows = sum(source.shape[1] for source in sources[::terms])
            shape = (sources[0].shape[0] // group, rows, sources[0].shape[2])
            body = functools.partial(add_split_kernel, shift, group, terms)
            cuts = kernel_call(body, [shape] * group, *sources)
            sources = [cuts[0]]
            for k in exchange_order(group):
                sources.append(swap(cuts[k], "row", rows_size, k << shift))
            terms = len(sources)
        return sources

    def scatter(sources, stages):
        return functools.reduce(jnp.add, exchanged(sources, stages))

    def gather(current):
        for shift, group in reversed(stages[2:]):
            blocks = [current] * group
            for k in exchange_order(group):
                blocks[k] = swap(current, "row", rows_size, k << shift)
            body = functools.partial(assemble_kernel, shift, group)
            shape = (current.shape[0] * group,) + current.shape[1:]
            (current,) = kernel_call(body, [shape], *blocks)
        shift, group = stages[1]
        blocks = [current]
        for k in exchange_order(group):
            blocks.append(swap(current, "row", rows_size, k << shift))
        return blocks + [swap(block, "row", rows_size, 1) for block in blocks]

    def per_device(vectors, panels, tfactors):
        col, row = lax.axis_index("col"), lax.axis_index("row")
        always = (row >> 16) == 0
        local_rows, eigvecs = vectors.shape
        own = panels.shape[2]
        width = own * cols_size
        out_cols = eigvecs // cols_size
        half = rows_size // 2
        near = max(1, rows_size // (2 * own))
        groups = cols_size // near
        count = 2 * near * own // rows_size
        packed = -(-(width // rows_size) * width // eigvecs)

        vt = panels.transpose(0, 2, 1)
        pieces = [None] * cols_size
        steps = list(range(cols_size - 1, 0, -1))
        for batch in (steps[:1], steps[1:] + [0]):
            for k in batch:
                at = turn(col, k, cols_size) * local_rows
                pieces[k] = lax.dynamic_slice_in_dim(vt, at, local_rows, 2)
            cuts, vt = lax.optimization_barrier(([pieces[k] for k in batch], vt))
            for k, cut in zip(batch, cuts):
                pairs = [(i, turn(i, k, cols_size)) for i in range(cols_size)]
                pieces[k] = lax.ppermute(cut, "col", pairs) if k else cut

        def early(distance, stages):
            part = [k for k in range(cols_size) if k % groups == distance]
            keep, send = kernel_call(
                functools.partial(near_kernel, rows_size, part, cols_size),
                [(half, count, eigvecs)] * 2,
                *[pieces[k] for k in part],
                vectors,
                scratch=[((2 * near * own, local_rows), bf16)] * 2,
            )
            return scatter([keep, swap(send, "row", rows_size, 1)], stages)

        bits = [(i, 2) for i in range(rows_size.bit_length() - 1)]
        same = lax.cond(
            always,
            functools.partial(early, 0, bits),
            lambda: jnp.zeros((1, count, eigvecs), jnp.float32),
        )

        def far(steps, rest, last):
            body = functools.partial(far_kernel, rows_size, steps, groups, rest, last, cols_size)
            rows = len(rest) * count + (packed if last else 0)
            keep, send, *house = kernel_call(
                body,
                [(half, rows, eigvecs)] * 2 + [(2, width, local_rows)] * last,
                *[pieces[k] for k in steps],
                vectors,
                scratch=[((2, width, local_rows), bf16)] * (2 * last)
                + [((2 * max(1, len(rest)) * near * own, local_rows), bf16)] * 2,
            )
            return [keep, swap(send, "row", rows_size, 1)], *house

        order = [k for k in range(groups - 1, groups // 2, -1)]
        sources = []
        others = [k for k in range(groups // 2, 0, -1)]
        for rest in (order, others):
            wanted = [k for k in range(1, cols_size) if k % groups in rest]
            cuts, (same, sources) = lax.optimization_barrier(
                ([pieces[k] for k in wanted], (same, sources))
            )
            for k, cut in zip(wanted, cuts):
                pieces[k] = cut
            if rest == order and order:
                (sources,) = far(wanted, rest, False)
        pair, house = far(steps + [0], others, True)
        order = order + others
        sources = exchanged(sources + pair, stages)
        sums = [same]
        (part,) = kernel_call(
            functools.partial(merge_kernel, cols_size, groups, order),
            [(1, groups * count + packed, eigvecs)],
            *sums,
            *sources,
            scratch=[((groups, count, eigvecs), jnp.float32)],
        )
        part, other = all_reduce_cols(part, rows_size, cols_size)

        blocks = kernel_call(
            functools.partial(
                tail_kernel, cols_size, groups, stages[1][0], [0] + exchange_order(stages[1][1])
            ),
            [(local_rows, out_cols)] * cols_size,
            *gather(part + other),
            tfactors,
            house,
            vectors,
            scratch=[((2 * width, eigvecs), jnp.float32), ((width, width), jnp.float32)],
        )
        blocks = list(blocks)
        for k in [3, 1, 2]:
            pairs = [(i, turn(i, k, cols_size)) for i in range(cols_size)]
            blocks[k] = lax.ppermute(blocks[k], "col", pairs)
        steps = [0, *range(cols_size - 1, 0, -2), *range(2, cols_size, 2)]
        out = pl.pallas_call(
            functools.partial(join_kernel, steps, cols_size),
            out_shape=jax.ShapeDtypeStruct((cols_size, local_rows, out_cols), jnp.float32),
            in_specs=[pl.BlockSpec(memory_space=pltpu.VMEM)] * cols_size,
            out_specs=pl.BlockSpec(memory_space=pl.ANY),
            scratch_shapes=[pltpu.SemaphoreType.DMA((cols_size,))],
            compiler_params=pltpu.CompilerParams(vmem_limit_bytes=4 * 1024 * 1024),
        )(*[blocks[k] for k in steps])
        return out.reshape((cols_size * local_rows, out_cols))

    return per_device


def solution(mesh):
    in_specs = (P(("row", "col"), None), P(None, "row", "col"), P())
    out_specs = P("row", "col")
    per_device = make_per_device(mesh.shape["row"], mesh.shape["col"])
    return jax.shard_map(
        per_device, mesh=mesh, in_specs=in_specs, out_specs=out_specs, check_vma=False
    )
```

```python
import functools

import jax
import jax.numpy as jnp
from jax import lax
from jax.experimental import pallas as pl
from jax.experimental.pallas import tpu as pltpu
from jax.sharding import PartitionSpec as P

PLAIN = ((1,), (0,))
BY_TRANSPOSE = ((1,), (1,))
FROM_TRANSPOSE = ((0,), (0,))


def split(value):
    high = value.astype(jnp.bfloat16)
    return high, (value - high.astype(jnp.float32)).astype(jnp.bfloat16)


def product(left, right, contract=PLAIN):
    def one(a, b):
        return lax.dot_general(a, b, (contract, ((), ())), preferred_element_type=jnp.float32)

    return one(left[0], right[0]) + (one(left[0], right[1]) + one(left[1], right[0]))


def here():
    return lax.axis_index("col"), lax.axis_index("row")


def kernel_call(body, shapes, *args, scratch=(), halves=()):
    return pl.pallas_call(
        body,
        out_shape=[jax.ShapeDtypeStruct(shape, jnp.float32) for shape in shapes]
        + [jax.ShapeDtypeStruct(shape, jnp.bfloat16) for shape in halves],
        in_specs=[pl.BlockSpec(memory_space=pltpu.VMEM)] * len(args),
        out_specs=[pl.BlockSpec(memory_space=pltpu.VMEM)] * (len(shapes) + len(halves)),
        scratch_shapes=[pltpu.VMEM(shape, kind) for shape, kind in scratch],
        compiler_params=pltpu.CompilerParams(vmem_limit_bytes=24 * 1024 * 1024),
    )(*args)


def swap(block, axis, size, mask):
    return lax.ppermute(block, axis, [(i, i ^ mask) for i in range(size)])


def row_stages(size):
    stages = []
    shift = 0
    while (1 << shift) < size:
        bits = 1 if shift == 0 or (2 << shift) == size else 2
        stages.append((shift, 1 << bits))
        shift += bits
    return stages


def exchange_order(group):
    return [2, 1, 3] if group == 4 else list(range(1, group))


def join_kernel(steps, cols_size, *refs):
    place, blocks, out, sem = here(), refs[: len(steps)], refs[-2], refs[-1]
    copies = []
    for i, (step, block) in enumerate(zip(steps, blocks)):
        source = turn(place[0], -step, cols_size)
        copies.append(pltpu.make_async_copy(block, out.at[source], sem.at[i]))
    for copy in copies:
        copy.start()
    for copy in copies:
        copy.wait()


def reverse(value, size):
    bits = size.bit_length() - 1
    return sum(((value >> i) & 1) << (bits - 1 - i) for i in range(bits))


def turn(col, step, size):
    return reverse((reverse(col, size) + step) & (size - 1), size)


def near_kernel(parts, steps, cols_size, *refs):
    place, pieces, (field, keep, send, high, low) = here(), refs[:-5], refs[-5:]
    col, core = place[0], place[1] & 1
    own, near = pieces[0].shape[1], len(pieces)
    for step, piece in zip(steps, pieces):
        at = pl.multiple_of((turn(col, -step, cols_size) & (near - 1)) * own, own)
        for panel in range(2):
            rows = pl.ds(panel * near * own + at, own)
            high[rows, :], low[rows, :] = split(piece[panel])
    result = product((high[...], low[...]), split(field[...]))
    for j in range(parts // 2):
        rows = keep.shape[1]
        even = result[2 * j * rows : (2 * j + 1) * rows]
        odd = result[(2 * j + 1) * rows : (2 * j + 2) * rows]
        keep[j] = jnp.where(core == 0, even, odd)
        send[j] = jnp.where(core == 0, odd, even)


def far_kernel(parts, steps, groups, rest, last, cols_size, *refs):
    place, pieces, refs = here(), refs[: len(steps)], refs[len(steps) :]
    if last:
        field, keep, send, high, low, far_h, far_l = refs
    else:
        field, keep, send, far_h, far_l = refs
    col, core = place[0], place[1] & 1
    own, near = pieces[0].shape[1], cols_size // groups
    for step, piece in zip(steps, pieces):
        block = turn(col, -step, cols_size)
        at = pl.multiple_of(block * own, own)
        inside = pl.multiple_of((block & (near - 1)) * own, own)
        for panel in range(2):
            value = piece[panel]
            rows = pl.ds(at, own)
            value_h, value_l = split(value)
            if last:
                high[panel, rows, :], low[panel, rows, :] = value_h, value_l
            if step % groups in rest:
                slot = 2 * rest.index(step % groups) + panel
                rows = pl.ds(inside + slot * near * own, own)
                far_h[rows, :], far_l[rows, :] = value_h, value_l
    if rest:
        result = product((far_h[...], far_l[...]), split(field[...]))
    height = 2 * near * own
    count = height // parts
    if last:
        cross = product((high[1], low[1]), (high[0], low[0]), BY_TRANSPOSE)
        rows = cross.shape[0] // parts
        side = keep.shape[2] // cross.shape[1]
        packed = -(-rows // side)
    for j in range(parts // 2):
        for out, odd in ((keep, core), (send, 1 - core)):

            def chosen(value, first, number, stride):
                even = value[first : first + number]
                return jnp.where(odd == 0, even, value[first + stride : first + stride + number])

            for slot in range(len(rest)):
                at = slot * count
                block = chosen(result, slot * height + 2 * j * count, count, count)
                out[j, at : at + count, :] = block
            if not last:
                continue
            at = len(rest) * count
            if packed * side != rows:
                out[j, at:, :] = jnp.zeros((packed, keep.shape[2]), jnp.float32)
            for i in range(rows // packed):
                block = chosen(cross, 2 * j * rows + i * packed, packed, rows)
                out[j, at:, i * cross.shape[1] : (i + 1) * cross.shape[1]] = block


def add_split_kernel(shift, group, terms, *refs):
    place, sources, outs = here(), refs[:-group], refs[-group:]
    me = (place[1] >> shift) & (group - 1)
    first = 0
    for i in range(0, len(sources), terms):
        rows = slice(first, first + sources[i].shape[1])
        first += sources[i].shape[1]
        for a in range(outs[0].shape[0]):
            for k, out in enumerate(outs):
                at = a * group + (me ^ k)
                total = sources[i][at]
                for source in sources[i + 1 : i + terms]:
                    total = total + source[at]
                out[a, rows] = total


def merge_kernel(cols_size, groups, order, *refs):
    place, early, sources = here(), refs[: groups - len(order)], refs[groups - len(order) : -2]
    out, scratch = refs[-2:]
    count = early[0].shape[1]
    total = sources[0][0]
    for source in sources[1:]:
        total = total + source[0]
    for distance, block in zip([d for d in range(groups) if d not in order], early):
        scratch[distance] = block[0]
    for i, distance in enumerate(order):
        scratch[distance] = total[i * count : (i + 1) * count]
    mine = reverse(place[0] // (cols_size // groups), groups)
    for group in range(groups):
        distance = (mine - reverse(group, groups)) & (groups - 1)
        out[0, group * count : (group + 1) * count] = scratch[distance]
    out[0, groups * count :] = total[len(order) * count :]


def assemble_kernel(shift, group, *refs):
    place, blocks, out = here(), refs[:-1], refs[-1]
    me = (place[1] >> shift) & (group - 1)
    for k, block in enumerate(blocks):
        for a in range(block.shape[0]):
            out[a * group + (me ^ k)] = block[a]


def tail_kernel(cols_size, groups, shift, ks, *refs):
    group = len(ks)
    place, blocks = here(), refs[: 2 * group]
    factors, high, low, field = refs[2 * group : 4 + 2 * group]
    outs, weights, cross = refs[4 + 2 * group : -2], refs[-2], refs[-1]
    col, core = place[0], place[1] & 1
    me = (place[1] >> shift) & (group - 1)
    width = high.shape[1]
    parts = 2 * group * blocks[0].shape[0]
    height = 2 * width // groups
    count = height // parts
    rows = width // parts
    packed = blocks[0].shape[1] - groups * count
    for i, block in enumerate(blocks):
        for a in range(block.shape[0]):
            p = 2 * (a * group + (me ^ ks[i % group])) + (core if i < group else 1 - core)
            start = p * count
            panel = start // (height // 2)
            start = panel * width + start - panel * (height // 2)
            for j in range(groups):
                at = pl.multiple_of(start + j * (height // 2), count)
                weights[pl.ds(at, count), :] = block[a, j * count : (j + 1) * count]
            for j in range(rows // packed):
                at = pl.multiple_of(p * rows + j * packed, packed)
                cut = slice(j * width, (j + 1) * width)
                cross[pl.ds(at, packed), :] = block[a, groups * count :, cut]

    first = split(product(split(factors[0]), split(weights[:width])))
    second = weights[width:] - product(split(cross[...]), first)
    second = split(product(split(factors[1]), split(second)))
    update = product((high[0], low[0]), first, FROM_TRANSPOSE)
    update = update + product((high[1], low[1]), second, FROM_TRANSPOSE)
    cols = outs[0].shape[1]
    result = field[...] - update
    for c in range(cols_size):
        for step, out in enumerate(outs):

            @pl.when(turn(col, step, cols_size) == c)
            def _(c=c, out=out):
                out[...] = result[:, c * cols : (c + 1) * cols]


def all_reduce_cols(part, rows_size, cols_size):
    bits = cols_size.bit_length() - 1
    for step in range(bits):
        pairs = []
        for row in range(rows_size):
            mask = 1 << (bits - 1 - step if row & 1 else step)
            for col in range(cols_size):
                pairs.append((row * cols_size + col, row * cols_size + (col ^ mask)))
        other = lax.ppermute(part, ("row", "col"), pairs)
        if step == bits - 1:
            return part, other
        part = part + other


def make_per_device(rows_size, cols_size):
    stages = row_stages(rows_size)
    bf16 = jnp.bfloat16

    def exchanged(sources, stages):
        terms = 2
        for shift, group in stages[1:]:
            rows = sum(source.shape[1] for source in sources[::terms])
            shape = (sources[0].shape[0] // group, rows, sources[0].shape[2])
            body = functools.partial(add_split_kernel, shift, group, terms)
            cuts = kernel_call(body, [shape] * group, *sources)
            sources = [cuts[0]]
            for k in exchange_order(group):
                sources.append(swap(cuts[k], "row", rows_size, k << shift))
            terms = len(sources)
        return sources

    def scatter(sources, stages):
        return functools.reduce(jnp.add, exchanged(sources, stages))

    def gather(current):
        for shift, group in reversed(stages[2:]):
            blocks = [current] * group
            for k in exchange_order(group):
                blocks[k] = swap(current, "row", rows_size, k << shift)
            body = functools.partial(assemble_kernel, shift, group)
            shape = (current.shape[0] * group,) + current.shape[1:]
            (current,) = kernel_call(body, [shape], *blocks)
        shift, group = stages[1]
        blocks = [current]
        for k in exchange_order(group):
            blocks.append(swap(current, "row", rows_size, k << shift))
        return blocks + [swap(block, "row", rows_size, 1) for block in blocks]

    def per_device(vectors, panels, tfactors):
        col, row = lax.axis_index("col"), lax.axis_index("row")
        always = (row >> 16) == 0
        local_rows, eigvecs = vectors.shape
        own = panels.shape[2]
        width = own * cols_size
        out_cols = eigvecs // cols_size
        half = rows_size // 2
        near = max(1, rows_size // (2 * own))
        groups = cols_size // near
        count = 2 * near * own // rows_size
        packed = -(-(width // rows_size) * width // eigvecs)

        vt = panels.transpose(0, 2, 1)
        pieces = [None] * cols_size
        steps = list(range(cols_size - 1, 0, -1))
        for batch in (steps[:1], steps[1:] + [0]):
            for k in batch:
                at = turn(col, k, cols_size) * local_rows
                pieces[k] = lax.dynamic_slice_in_dim(vt, at, local_rows, 2)
            cuts, vt = lax.optimization_barrier(([pieces[k] for k in batch], vt))
            for k, cut in zip(batch, cuts):
                pairs = [(i, turn(i, k, cols_size)) for i in range(cols_size)]
                pieces[k] = lax.ppermute(cut, "col", pairs) if k else cut

        def early(distance, stages):
            part = [k for k in range(cols_size) if k % groups == distance]
            keep, send = kernel_call(
                functools.partial(near_kernel, rows_size, part, cols_size),
                [(half, count, eigvecs)] * 2,
                *[pieces[k] for k in part],
                vectors,
                scratch=[((2 * near * own, local_rows), bf16)] * 2,
            )
            return scatter([keep, swap(send, "row", rows_size, 1)], stages)

        bits = [(i, 2) for i in range(rows_size.bit_length() - 1)]
        same = lax.cond(
            always,
            functools.partial(early, 0, bits),
            lambda: jnp.zeros((1, count, eigvecs), jnp.float32),
        )

        def far(steps, rest, last):
            body = functools.partial(far_kernel, rows_size, steps, groups, rest, last, cols_size)
            rows = len(rest) * count + (packed if last else 0)
            keep, send, *house = kernel_call(
                body,
                [(half, rows, eigvecs)] * 2,
                *[pieces[k] for k in steps],
                vectors,
                scratch=[((2 * max(1, len(rest)) * near * own, local_rows), bf16)] * 2,
                halves=[(2, width, local_rows)] * (2 * last),
            )
            return [keep, swap(send, "row", rows_size, 1)], *house

        order = [k for k in range(groups - 1, groups // 2, -1)]
        sources = []
        others = [k for k in range(groups // 2, 0, -1)]
        for rest in (order, others):
            wanted = [k for k in range(1, cols_size) if k % groups in rest]
            cuts, (same, sources) = lax.optimization_barrier(
                ([pieces[k] for k in wanted], (same, sources))
            )
            for k, cut in zip(wanted, cuts):
                pieces[k] = cut
            if rest == order and order:
                (sources,) = far(wanted, rest, False)
        pair, *house = far(steps + [0], others, True)
        order = order + others
        sources = exchanged(sources + pair, stages)
        sums = [same]
        (part,) = kernel_call(
            functools.partial(merge_kernel, cols_size, groups, order),
            [(1, groups * count + packed, eigvecs)],
            *sums,
            *sources,
            scratch=[((groups, count, eigvecs), jnp.float32)],
        )
        part, other = all_reduce_cols(part, rows_size, cols_size)

        blocks = kernel_call(
            functools.partial(
                tail_kernel, cols_size, groups, stages[1][0], [0] + exchange_order(stages[1][1])
            ),
            [(local_rows, out_cols)] * cols_size,
            *gather(part + other),
            tfactors,
            *house,
            vectors,
            scratch=[((2 * width, eigvecs), jnp.float32), ((width, width), jnp.float32)],
        )
        blocks = list(blocks)
        for k in [3, 1, 2]:
            pairs = [(i, turn(i, k, cols_size)) for i in range(cols_size)]
            blocks[k] = lax.ppermute(blocks[k], "col", pairs)
        steps = [0, *range(cols_size - 1, 0, -2), *range(2, cols_size, 2)]
        out = pl.pallas_call(
            functools.partial(join_kernel, steps, cols_size),
            out_shape=jax.ShapeDtypeStruct((cols_size, local_rows, out_cols), jnp.float32),
            in_specs=[pl.BlockSpec(memory_space=pltpu.VMEM)] * cols_size,
            out_specs=pl.BlockSpec(memory_space=pl.ANY),
            scratch_shapes=[pltpu.SemaphoreType.DMA((cols_size,))],
            compiler_params=pltpu.CompilerParams(vmem_limit_bytes=4 * 1024 * 1024),
        )(*[blocks[k] for k in steps])
        return out.reshape((cols_size * local_rows, out_cols))

    return per_device


def solution(mesh):
    in_specs = (P(("row", "col"), None), P(None, "row", "col"), P())
    out_specs = P("row", "col")
    per_device = make_per_device(mesh.shape["row"], mesh.shape["col"])
    return jax.shard_map(
        per_device, mesh=mesh, in_specs=in_specs, out_specs=out_specs, check_vma=False
    )
```

```python
import functools

import jax
import jax.numpy as jnp
from jax import lax
from jax.experimental import pallas as pl
from jax.experimental.pallas import tpu as pltpu
from jax.sharding import PartitionSpec as P

PLAIN = ((1,), (0,))
BY_TRANSPOSE = ((1,), (1,))
FROM_TRANSPOSE = ((0,), (0,))


def split(value):
    high = value.astype(jnp.bfloat16)
    return high, (value - high.astype(jnp.float32)).astype(jnp.bfloat16)


def product(left, right, contract=PLAIN):
    def one(a, b):
        return lax.dot_general(a, b, (contract, ((), ())), preferred_element_type=jnp.float32)

    return one(left[0], right[0]) + (one(left[0], right[1]) + one(left[1], right[0]))


def joined(left, right, contract=PLAIN):
    (i,), (j,) = contract
    left = jnp.concatenate([left[0], left[1], left[0]], i)
    right = jnp.concatenate([right[0], right[0], right[1]], j)
    return lax.dot_general(left, right, (contract, ((), ())), preferred_element_type=jnp.float32)


def here():
    return lax.axis_index("col"), lax.axis_index("row")


def kernel_call(body, shapes, *args, scratch=(), halves=()):
    return pl.pallas_call(
        body,
        out_shape=[jax.ShapeDtypeStruct(shape, jnp.float32) for shape in shapes]
        + [jax.ShapeDtypeStruct(shape, jnp.bfloat16) for shape in halves],
        in_specs=[pl.BlockSpec(memory_space=pltpu.VMEM)] * len(args),
        out_specs=[pl.BlockSpec(memory_space=pltpu.VMEM)] * (len(shapes) + len(halves)),
        scratch_shapes=[pltpu.VMEM(shape, kind) for shape, kind in scratch],
        compiler_params=pltpu.CompilerParams(vmem_limit_bytes=24 * 1024 * 1024),
    )(*args)


def swap(block, axis, size, mask):
    return lax.ppermute(block, axis, [(i, i ^ mask) for i in range(size)])


def row_stages(size):
    stages = []
    shift = 0
    while (1 << shift) < size:
        bits = 1 if shift == 0 or (2 << shift) == size else 2
        stages.append((shift, 1 << bits))
        shift += bits
    return stages


def exchange_order(group):
    return [2, 1, 3] if group == 4 else list(range(1, group))


def join_kernel(steps, cols_size, *refs):
    place, blocks, out, sem = here(), refs[: len(steps)], refs[-2], refs[-1]
    copies = []
    for i, (step, block) in enumerate(zip(steps, blocks)):
        source = turn(place[0], -step, cols_size)
        copies.append(pltpu.make_async_copy(block, out.at[source], sem.at[i]))
    for copy in copies:
        copy.start()
    for copy in copies:
        copy.wait()


def reverse(value, size):
    bits = size.bit_length() - 1
    return sum(((value >> i) & 1) << (bits - 1 - i) for i in range(bits))


def turn(col, step, size):
    return reverse((reverse(col, size) + step) & (size - 1), size)


def near_kernel(parts, steps, cols_size, *refs):
    place, pieces, (field, keep, send, high, low) = here(), refs[:-5], refs[-5:]
    col, core = place[0], place[1] & 1
    own, near = pieces[0].shape[1], len(pieces)
    for step, piece in zip(steps, pieces):
        at = pl.multiple_of((turn(col, -step, cols_size) & (near - 1)) * own, own)
        for panel in range(2):
            rows = pl.ds(panel * near * own + at, own)
            high[rows, :], low[rows, :] = split(piece[panel])
    result = joined((high[...], low[...]), split(field[...]))
    for j in range(parts // 2):
        rows = keep.shape[1]
        even = result[2 * j * rows : (2 * j + 1) * rows]
        odd = result[(2 * j + 1) * rows : (2 * j + 2) * rows]
        keep[j] = jnp.where(core == 0, even, odd)
        send[j] = jnp.where(core == 0, odd, even)


def far_kernel(parts, steps, groups, rest, last, cols_size, *refs):
    place, pieces, refs = here(), refs[: len(steps)], refs[len(steps) :]
    if last:
        field, keep, send, high, low, far_h, far_l = refs
    else:
        field, keep, send, far_h, far_l = refs
    col, core = place[0], place[1] & 1
    own, near = pieces[0].shape[1], cols_size // groups
    for step, piece in zip(steps, pieces):
        block = turn(col, -step, cols_size)
        at = pl.multiple_of(block * own, own)
        inside = pl.multiple_of((block & (near - 1)) * own, own)
        for panel in range(2):
            value = piece[panel]
            rows = pl.ds(at, own)
            value_h, value_l = split(value)
            if last:
                high[panel, rows, :], low[panel, rows, :] = value_h, value_l
            if step % groups in rest:
                slot = 2 * rest.index(step % groups) + panel
                rows = pl.ds(inside + slot * near * own, own)
                far_h[rows, :], far_l[rows, :] = value_h, value_l
    if rest:
        result = joined((far_h[...], far_l[...]), split(field[...]))
    height = 2 * near * own
    count = height // parts
    if last:
        cross = joined((high[1], low[1]), (high[0], low[0]), BY_TRANSPOSE)
        rows = cross.shape[0] // parts
        side = keep.shape[2] // cross.shape[1]
        packed = -(-rows // side)
    for j in range(parts // 2):
        for out, odd in ((keep, core), (send, 1 - core)):

            def chosen(value, first, number, stride):
                even = value[first : first + number]
                return jnp.where(odd == 0, even, value[first + stride : first + stride + number])

            for slot in range(len(rest)):
                at = slot * count
                block = chosen(result, slot * height + 2 * j * count, count, count)
                out[j, at : at + count, :] = block
            if not last:
                continue
            at = len(rest) * count
            if packed * side != rows:
                out[j, at:, :] = jnp.zeros((packed, keep.shape[2]), jnp.float32)
            for i in range(rows // packed):
                block = chosen(cross, 2 * j * rows + i * packed, packed, rows)
                out[j, at:, i * cross.shape[1] : (i + 1) * cross.shape[1]] = block


def add_split_kernel(shift, group, terms, *refs):
    place, sources, outs = here(), refs[:-group], refs[-group:]
    me = (place[1] >> shift) & (group - 1)
    first = 0
    for i in range(0, len(sources), terms):
        rows = slice(first, first + sources[i].shape[1])
        first += sources[i].shape[1]
        for a in range(outs[0].shape[0]):
            for k, out in enumerate(outs):
                at = a * group + (me ^ k)
                total = sources[i][at]
                for source in sources[i + 1 : i + terms]:
                    total = total + source[at]
                out[a, rows] = total


def merge_kernel(cols_size, groups, order, *refs):
    place, early, sources = here(), refs[: groups - len(order)], refs[groups - len(order) : -2]
    out, scratch = refs[-2:]
    count = early[0].shape[1]
    total = sources[0][0]
    for source in sources[1:]:
        total = total + source[0]
    for distance, block in zip([d for d in range(groups) if d not in order], early):
        scratch[distance] = block[0]
    for i, distance in enumerate(order):
        scratch[distance] = total[i * count : (i + 1) * count]
    mine = reverse(place[0] // (cols_size // groups), groups)
    for group in range(groups):
        distance = (mine - reverse(group, groups)) & (groups - 1)
        out[0, group * count : (group + 1) * count] = scratch[distance]
    out[0, groups * count :] = total[len(order) * count :]


def assemble_kernel(shift, group, *refs):
    place, blocks, out = here(), refs[:-1], refs[-1]
    me = (place[1] >> shift) & (group - 1)
    for k, block in enumerate(blocks):
        for a in range(block.shape[0]):
            out[a * group + (me ^ k)] = block[a]


def tail_kernel(cols_size, groups, shift, ks, *refs):
    group = len(ks)
    place, blocks = here(), refs[: 2 * group]
    factors, high, low, field = refs[2 * group : 4 + 2 * group]
    outs, weights, cross = refs[4 + 2 * group : -2], refs[-2], refs[-1]
    col, core = place[0], place[1] & 1
    me = (place[1] >> shift) & (group - 1)
    width = high.shape[1]
    parts = 2 * group * blocks[0].shape[0]
    height = 2 * width // groups
    count = height // parts
    rows = width // parts
    packed = blocks[0].shape[1] - groups * count
    for i, block in enumerate(blocks):
        for a in range(block.shape[0]):
            p = 2 * (a * group + (me ^ ks[i % group])) + (core if i < group else 1 - core)
            start = p * count
            panel = start // (height // 2)
            start = panel * width + start - panel * (height // 2)
            for j in range(groups):
                at = pl.multiple_of(start + j * (height // 2), count)
                weights[pl.ds(at, count), :] = block[a, j * count : (j + 1) * count]
            for j in range(rows // packed):
                at = pl.multiple_of(p * rows + j * packed, packed)
                cut = slice(j * width, (j + 1) * width)
                cross[pl.ds(at, packed), :] = block[a, groups * count :, cut]

    first = split(product(split(factors[0]), split(weights[:width])))
    second = weights[width:] - product(split(cross[...]), first)
    second = split(product(split(factors[1]), split(second)))
    update = product((high[0], low[0]), first, FROM_TRANSPOSE)
    update = update + product((high[1], low[1]), second, FROM_TRANSPOSE)
    cols = outs[0].shape[1]
    result = field[...] - update
    for c in range(cols_size):
        for step, out in enumerate(outs):

            @pl.when(turn(col, step, cols_size) == c)
            def _(c=c, out=out):
                out[...] = result[:, c * cols : (c + 1) * cols]


def all_reduce_cols(part, rows_size, cols_size):
    bits = cols_size.bit_length() - 1
    for step in range(bits):
        pairs = []
        for row in range(rows_size):
            mask = 1 << (bits - 1 - step if row & 1 else step)
            for col in range(cols_size):
                pairs.append((row * cols_size + col, row * cols_size + (col ^ mask)))
        other = lax.ppermute(part, ("row", "col"), pairs)
        if step == bits - 1:
            return part, other
        part = part + other


def make_per_device(rows_size, cols_size):
    stages = row_stages(rows_size)
    bf16 = jnp.bfloat16

    def exchanged(sources, stages):
        terms = 2
        for shift, group in stages[1:]:
            rows = sum(source.shape[1] for source in sources[::terms])
            shape = (sources[0].shape[0] // group, rows, sources[0].shape[2])
            body = functools.partial(add_split_kernel, shift, group, terms)
            cuts = kernel_call(body, [shape] * group, *sources)
            sources = [cuts[0]]
            for k in exchange_order(group):
                sources.append(swap(cuts[k], "row", rows_size, k << shift))
            terms = len(sources)
        return sources

    def scatter(sources, stages):
        return functools.reduce(jnp.add, exchanged(sources, stages))

    def gather(current):
        for shift, group in reversed(stages[2:]):
            blocks = [current] * group
            for k in exchange_order(group):
                blocks[k] = swap(current, "row", rows_size, k << shift)
            body = functools.partial(assemble_kernel, shift, group)
            shape = (current.shape[0] * group,) + current.shape[1:]
            (current,) = kernel_call(body, [shape], *blocks)
        shift, group = stages[1]
        blocks = [current]
        for k in exchange_order(group):
            blocks.append(swap(current, "row", rows_size, k << shift))
        return blocks + [swap(block, "row", rows_size, 1) for block in blocks]

    def per_device(vectors, panels, tfactors):
        col, row = lax.axis_index("col"), lax.axis_index("row")
        always = (row >> 16) == 0
        local_rows, eigvecs = vectors.shape
        own = panels.shape[2]
        width = own * cols_size
        out_cols = eigvecs // cols_size
        half = rows_size // 2
        near = max(1, rows_size // (2 * own))
        groups = cols_size // near
        count = 2 * near * own // rows_size
        packed = -(-(width // rows_size) * width // eigvecs)

        vt = panels.transpose(0, 2, 1)
        pieces = [None] * cols_size
        steps = list(range(cols_size - 1, 0, -1))
        for batch in (steps[:1], steps[1:] + [0]):
            for k in batch:
                at = turn(col, k, cols_size) * local_rows
                pieces[k] = lax.dynamic_slice_in_dim(vt, at, local_rows, 2)
            cuts, vt = lax.optimization_barrier(([pieces[k] for k in batch], vt))
            for k, cut in zip(batch, cuts):
                pairs = [(i, turn(i, k, cols_size)) for i in range(cols_size)]
                pieces[k] = lax.ppermute(cut, "col", pairs) if k else cut

        def early(distance, stages):
            part = [k for k in range(cols_size) if k % groups == distance]
            keep, send = kernel_call(
                functools.partial(near_kernel, rows_size, part, cols_size),
                [(half, count, eigvecs)] * 2,
                *[pieces[k] for k in part],
                vectors,
                scratch=[((2 * near * own, local_rows), bf16)] * 2,
            )
            return scatter([keep, swap(send, "row", rows_size, 1)], stages)

        bits = [(i, 2) for i in range(rows_size.bit_length() - 1)]
        same = lax.cond(
            always,
            functools.partial(early, 0, bits),
            lambda: jnp.zeros((1, count, eigvecs), jnp.float32),
        )

        def far(steps, rest, last):
            body = functools.partial(far_kernel, rows_size, steps, groups, rest, last, cols_size)
            rows = len(rest) * count + (packed if last else 0)
            keep, send, *house = kernel_call(
                body,
                [(half, rows, eigvecs)] * 2,
                *[pieces[k] for k in steps],
                vectors,
                scratch=[((2 * max(1, len(rest)) * near * own, local_rows), bf16)] * 2,
                halves=[(2, width, local_rows)] * (2 * last),
            )
            return [keep, swap(send, "row", rows_size, 1)], *house

        order = [k for k in range(groups - 1, groups // 2, -1)]
        sources = []
        others = [k for k in range(groups // 2, 0, -1)]
        for rest in (order, others):
            wanted = [k for k in range(1, cols_size) if k % groups in rest]
            cuts, (same, sources) = lax.optimization_barrier(
                ([pieces[k] for k in wanted], (same, sources))
            )
            for k, cut in zip(wanted, cuts):
                pieces[k] = cut
            if rest == order and order:
                (sources,) = far(wanted, rest, False)
        pair, *house = far(steps + [0], others, True)
        order = order + others
        sources = exchanged(sources + pair, stages)
        sums = [same]
        (part,) = kernel_call(
            functools.partial(merge_kernel, cols_size, groups, order),
            [(1, groups * count + packed, eigvecs)],
            *sums,
            *sources,
            scratch=[((groups, count, eigvecs), jnp.float32)],
        )
        part, other = all_reduce_cols(part, rows_size, cols_size)

        blocks = kernel_call(
            functools.partial(
                tail_kernel, cols_size, groups, stages[1][0], [0] + exchange_order(stages[1][1])
            ),
            [(local_rows, out_cols)] * cols_size,
            *gather(part + other),
            tfactors,
            *house,
            vectors,
            scratch=[((2 * width, eigvecs), jnp.float32), ((width, width), jnp.float32)],
        )
        blocks = list(blocks)
        for k in [3, 1, 2]:
            pairs = [(i, turn(i, k, cols_size)) for i in range(cols_size)]
            blocks[k] = lax.ppermute(blocks[k], "col", pairs)
        steps = [0, *range(cols_size - 1, 0, -2), *range(2, cols_size, 2)]
        out = pl.pallas_call(
            functools.partial(join_kernel, steps, cols_size),
            out_shape=jax.ShapeDtypeStruct((cols_size, local_rows, out_cols), jnp.float32),
            in_specs=[pl.BlockSpec(memory_space=pltpu.VMEM)] * cols_size,
            out_specs=pl.BlockSpec(memory_space=pl.ANY),
            scratch_shapes=[pltpu.SemaphoreType.DMA((cols_size,))],
            compiler_params=pltpu.CompilerParams(vmem_limit_bytes=4 * 1024 * 1024),
        )(*[blocks[k] for k in steps])
        return out.reshape((cols_size * local_rows, out_cols))

    return per_device


def solution(mesh):
    in_specs = (P(("row", "col"), None), P(None, "row", "col"), P())
    out_specs = P("row", "col")
    per_device = make_per_device(mesh.shape["row"], mesh.shape["col"])
    return jax.shard_map(
        per_device, mesh=mesh, in_specs=in_specs, out_specs=out_specs, check_vma=False
    )
```

```python
import functools

import jax
import jax.numpy as jnp
from jax import lax
from jax.experimental import pallas as pl
from jax.experimental.pallas import tpu as pltpu
from jax.sharding import PartitionSpec as P

PLAIN = ((1,), (0,))
BY_TRANSPOSE = ((1,), (1,))
FROM_TRANSPOSE = ((0,), (0,))


def split(value):
    high = value.astype(jnp.bfloat16)
    return high, (value - high.astype(jnp.float32)).astype(jnp.bfloat16)


def product(left, right, contract=PLAIN):
    def one(a, b):
        return lax.dot_general(a, b, (contract, ((), ())), preferred_element_type=jnp.float32)

    return one(left[0], right[0]) + (one(left[0], right[1]) + one(left[1], right[0]))


def here():
    return lax.axis_index("col"), lax.axis_index("row")


def kernel_call(body, shapes, *args, scratch=(), halves=()):
    return pl.pallas_call(
        body,
        out_shape=[jax.ShapeDtypeStruct(shape, jnp.float32) for shape in shapes]
        + [jax.ShapeDtypeStruct(shape, jnp.bfloat16) for shape in halves],
        in_specs=[pl.BlockSpec(memory_space=pltpu.VMEM)] * len(args),
        out_specs=[pl.BlockSpec(memory_space=pltpu.VMEM)] * (len(shapes) + len(halves)),
        scratch_shapes=[pltpu.VMEM(shape, kind) for shape, kind in scratch],
        compiler_params=pltpu.CompilerParams(vmem_limit_bytes=24 * 1024 * 1024),
    )(*args)


def swap(block, axis, size, mask):
    return lax.ppermute(block, axis, [(i, i ^ mask) for i in range(size)])


def row_stages(size):
    stages = []
    shift = 0
    while (1 << shift) < size:
        bits = 1 if shift == 0 or (2 << shift) == size else 2
        stages.append((shift, 1 << bits))
        shift += bits
    return stages


def exchange_order(group):
    return [2, 1, 3] if group == 4 else list(range(1, group))


def join_kernel(steps, cols_size, *refs):
    place, blocks, out, sem = here(), refs[: len(steps)], refs[-2], refs[-1]
    copies = []
    for i, (step, block) in enumerate(zip(steps, blocks)):
        source = turn(place[0], -step, cols_size)
        copies.append(pltpu.make_async_copy(block, out.at[source], sem.at[i]))
    for copy in copies:
        copy.start()
    for copy in copies:
        copy.wait()


def reverse(value, size):
    bits = size.bit_length() - 1
    return sum(((value >> i) & 1) << (bits - 1 - i) for i in range(bits))


def turn(col, step, size):
    return reverse((reverse(col, size) + step) & (size - 1), size)


def near_kernel(parts, steps, cols_size, *refs):
    place, pieces, (field, keep, send, high, low) = here(), refs[:-5], refs[-5:]
    col, core = place[0], place[1] & 1
    own, near = pieces[0].shape[1], len(pieces)
    for step, piece in zip(steps, pieces):
        at = pl.multiple_of((turn(col, -step, cols_size) & (near - 1)) * own, own)
        for panel in range(2):
            rows = pl.ds(panel * near * own + at, own)
            high[rows, :], low[rows, :] = split(piece[panel])
    result = product((high[...], low[...]), split(field[...]))
    for j in range(parts // 2):
        rows = keep.shape[1]
        even = result[2 * j * rows : (2 * j + 1) * rows]
        odd = result[(2 * j + 1) * rows : (2 * j + 2) * rows]
        keep[j] = jnp.where(core == 0, even, odd)
        send[j] = jnp.where(core == 0, odd, even)


def far_kernel(parts, steps, groups, rest, last, cols_size, *refs):
    place, pieces, refs = here(), refs[: len(steps)], refs[len(steps) :]
    if last:
        field, keep, send, high, low, far_h, far_l = refs
    else:
        field, keep, send, far_h, far_l = refs
    col, core = place[0], place[1] & 1
    own, near = pieces[0].shape[1], cols_size // groups
    for step, piece in zip(steps, pieces):
        block = turn(col, -step, cols_size)
        at = pl.multiple_of(block * own, own)
        inside = pl.multiple_of((block & (near - 1)) * own, own)
        for panel in range(2):
            value = piece[panel]
            rows = pl.ds(at, own)
            value_h, value_l = split(value)
            if last:
                high[panel, rows, :], low[panel, rows, :] = value_h, value_l
            if step % groups in rest:
                slot = 2 * rest.index(step % groups) + panel
                rows = pl.ds(inside + slot * near * own, own)
                far_h[rows, :], far_l[rows, :] = value_h, value_l
    if rest:
        result = product((far_h[...], far_l[...]), split(field[...]))
    height = 2 * near * own
    count = height // parts
    if last:
        cross = product((high[1], low[1]), (high[0], low[0]), BY_TRANSPOSE)
        rows = cross.shape[0] // parts
        side = keep.shape[2] // cross.shape[1]
        packed = -(-rows // side)
    for j in range(parts // 2):
        for out, odd in ((keep, core), (send, 1 - core)):

            def chosen(value, first, number, stride):
                even = value[first : first + number]
                return jnp.where(odd == 0, even, value[first + stride : first + stride + number])

            for slot in range(len(rest)):
                at = slot * count
                block = chosen(result, slot * height + 2 * j * count, count, count)
                out[j, at : at + count, :] = block
            if not last:
                continue
            at = len(rest) * count
            if packed * side != rows:
                out[j, at:, :] = jnp.zeros((packed, keep.shape[2]), jnp.float32)
            for i in range(rows // packed):
                block = chosen(cross, 2 * j * rows + i * packed, packed, rows)
                out[j, at:, i * cross.shape[1] : (i + 1) * cross.shape[1]] = block


def add_split_kernel(shift, group, terms, *refs):
    place, sources, outs = here(), refs[:-group], refs[-group:]
    me = (place[1] >> shift) & (group - 1)
    first = 0
    for i in range(0, len(sources), terms):
        rows = slice(first, first + sources[i].shape[1])
        first += sources[i].shape[1]
        for a in range(outs[0].shape[0]):
            for k, out in enumerate(outs):
                at = a * group + (me ^ k)
                total = sources[i][at]
                for source in sources[i + 1 : i + terms]:
                    total = total + source[at]
                out[a, rows] = total


def merge_kernel(cols_size, groups, order, *refs):
    place, early, sources = here(), refs[: groups - len(order)], refs[groups - len(order) : -2]
    out, scratch = refs[-2:]
    count = early[0].shape[1]
    total = sources[0][0]
    for source in sources[1:]:
        total = total + source[0]
    for distance, block in zip([d for d in range(groups) if d not in order], early):
        scratch[distance] = block[0]
    for i, distance in enumerate(order):
        scratch[distance] = total[i * count : (i + 1) * count]
    mine = reverse(place[0] // (cols_size // groups), groups)
    for group in range(groups):
        distance = (mine - reverse(group, groups)) & (groups - 1)
        out[0, group * count : (group + 1) * count] = scratch[distance]
    out[0, groups * count :] = total[len(order) * count :]


def add_kernel(left, right, out):
    out[...] = left[...] + right[...]


def assemble_kernel(shift, group, *refs):
    place, blocks, out = here(), refs[:-1], refs[-1]
    me = (place[1] >> shift) & (group - 1)
    for k, block in enumerate(blocks):
        for a in range(block.shape[0]):
            out[a * group + (me ^ k)] = block[a]


def tail_kernel(cols_size, groups, shift, ks, *refs):
    group = len(ks)
    place, blocks = here(), refs[: 2 * group]
    factors, high, low, field = refs[2 * group : 4 + 2 * group]
    outs, weights, cross = refs[4 + 2 * group : -2], refs[-2], refs[-1]
    col, core = place[0], place[1] & 1
    me = (place[1] >> shift) & (group - 1)
    width = high.shape[1]
    parts = 2 * group * blocks[0].shape[0]
    height = 2 * width // groups
    count = height // parts
    rows = width // parts
    packed = blocks[0].shape[1] - groups * count
    for i, block in enumerate(blocks):
        for a in range(block.shape[0]):
            p = 2 * (a * group + (me ^ ks[i % group])) + (core if i < group else 1 - core)
            start = p * count
            panel = start // (height // 2)
            start = panel * width + start - panel * (height // 2)
            for j in range(groups):
                at = pl.multiple_of(start + j * (height // 2), count)
                weights[pl.ds(at, count), :] = block[a, j * count : (j + 1) * count]
            for j in range(rows // packed):
                at = pl.multiple_of(p * rows + j * packed, packed)
                cut = slice(j * width, (j + 1) * width)
                cross[pl.ds(at, packed), :] = block[a, groups * count :, cut]

    first = split(product(split(factors[0]), split(weights[:width])))
    second = weights[width:] - product(split(cross[...]), first)
    second = split(product(split(factors[1]), split(second)))
    update = product((high[0], low[0]), first, FROM_TRANSPOSE)
    update = update + product((high[1], low[1]), second, FROM_TRANSPOSE)
    cols = outs[0].shape[1]
    result = field[...] - update
    for c in range(cols_size):
        for step, out in enumerate(outs):

            @pl.when(turn(col, step, cols_size) == c)
            def _(c=c, out=out):
                out[...] = result[:, c * cols : (c + 1) * cols]


def all_reduce_cols(part, rows_size, cols_size):
    bits = cols_size.bit_length() - 1
    for step in range(bits):
        pairs = []
        for row in range(rows_size):
            mask = 1 << (bits - 1 - step if row & 1 else step)
            for col in range(cols_size):
                pairs.append((row * cols_size + col, row * cols_size + (col ^ mask)))
        other = lax.ppermute(part, ("row", "col"), pairs)
        if step == bits - 1:
            return part, other
        (part,) = kernel_call(add_kernel, [part.shape], part, other)


def make_per_device(rows_size, cols_size):
    stages = row_stages(rows_size)
    bf16 = jnp.bfloat16

    def exchanged(sources, stages):
        terms = 2
        for shift, group in stages[1:]:
            rows = sum(source.shape[1] for source in sources[::terms])
            shape = (sources[0].shape[0] // group, rows, sources[0].shape[2])
            body = functools.partial(add_split_kernel, shift, group, terms)
            cuts = kernel_call(body, [shape] * group, *sources)
            sources = [cuts[0]]
            for k in exchange_order(group):
                sources.append(swap(cuts[k], "row", rows_size, k << shift))
            terms = len(sources)
        return sources

    def scatter(sources, stages):
        return functools.reduce(jnp.add, exchanged(sources, stages))

    def gather(current):
        for shift, group in reversed(stages[2:]):
            blocks = [current] * group
            for k in exchange_order(group):
                blocks[k] = swap(current, "row", rows_size, k << shift)
            body = functools.partial(assemble_kernel, shift, group)
            shape = (current.shape[0] * group,) + current.shape[1:]
            (current,) = kernel_call(body, [shape], *blocks)
        shift, group = stages[1]
        blocks = [current]
        for k in exchange_order(group):
            blocks.append(swap(current, "row", rows_size, k << shift))
        return blocks + [swap(block, "row", rows_size, 1) for block in blocks]

    def per_device(vectors, panels, tfactors):
        col, row = lax.axis_index("col"), lax.axis_index("row")
        always = (row >> 16) == 0
        local_rows, eigvecs = vectors.shape
        own = panels.shape[2]
        width = own * cols_size
        out_cols = eigvecs // cols_size
        half = rows_size // 2
        near = max(1, rows_size // (2 * own))
        groups = cols_size // near
        count = 2 * near * own // rows_size
        packed = -(-(width // rows_size) * width // eigvecs)

        vt = panels.transpose(0, 2, 1)
        pieces = [None] * cols_size
        steps = list(range(cols_size - 1, 0, -1))
        for batch in (steps[:1], steps[1:] + [0]):
            for k in batch:
                at = turn(col, k, cols_size) * local_rows
                pieces[k] = lax.dynamic_slice_in_dim(vt, at, local_rows, 2)
            cuts, vt = lax.optimization_barrier(([pieces[k] for k in batch], vt))
            for k, cut in zip(batch, cuts):
                pairs = [(i, turn(i, k, cols_size)) for i in range(cols_size)]
                pieces[k] = lax.ppermute(cut, "col", pairs) if k else cut

        def early(distance, stages):
            part = [k for k in range(cols_size) if k % groups == distance]
            keep, send = kernel_call(
                functools.partial(near_kernel, rows_size, part, cols_size),
                [(half, count, eigvecs)] * 2,
                *[pieces[k] for k in part],
                vectors,
                scratch=[((2 * near * own, local_rows), bf16)] * 2,
            )
            return scatter([keep, swap(send, "row", rows_size, 1)], stages)

        bits = [(i, 2) for i in range(rows_size.bit_length() - 1)]
        same = lax.cond(
            always,
            functools.partial(early, 0, bits),
            lambda: jnp.zeros((1, count, eigvecs), jnp.float32),
        )

        def far(steps, rest, last):
            body = functools.partial(far_kernel, rows_size, steps, groups, rest, last, cols_size)
            rows = len(rest) * count + (packed if last else 0)
            keep, send, *house = kernel_call(
                body,
                [(half, rows, eigvecs)] * 2,
                *[pieces[k] for k in steps],
                vectors,
                scratch=[((2 * max(1, len(rest)) * near * own, local_rows), bf16)] * 2,
                halves=[(2, width, local_rows)] * (2 * last),
            )
            return [keep, swap(send, "row", rows_size, 1)], *house

        order = [k for k in range(groups - 1, groups // 2, -1)]
        sources = []
        others = [k for k in range(groups // 2, 0, -1)]
        for rest in (order, others):
            wanted = [k for k in range(1, cols_size) if k % groups in rest]
            cuts, (same, sources) = lax.optimization_barrier(
                ([pieces[k] for k in wanted], (same, sources))
            )
            for k, cut in zip(wanted, cuts):
                pieces[k] = cut
            if rest == order and order:
                (sources,) = far(wanted, rest, False)
        pair, *house = far(steps + [0], others, True)
        order = order + others
        sources = exchanged(sources + pair, stages)
        sums = [same]
        (part,) = kernel_call(
            functools.partial(merge_kernel, cols_size, groups, order),
            [(1, groups * count + packed, eigvecs)],
            *sums,
            *sources,
            scratch=[((groups, count, eigvecs), jnp.float32)],
        )
        part, other = all_reduce_cols(part, rows_size, cols_size)

        blocks = kernel_call(
            functools.partial(
                tail_kernel, cols_size, groups, stages[1][0], [0] + exchange_order(stages[1][1])
            ),
            [(local_rows, out_cols)] * cols_size,
            *gather(kernel_call(add_kernel, [part.shape], part, other)[0]),
            tfactors,
            *house,
            vectors,
            scratch=[((2 * width, eigvecs), jnp.float32), ((width, width), jnp.float32)],
        )
        blocks = list(blocks)
        for k in [3, 1, 2]:
            pairs = [(i, turn(i, k, cols_size)) for i in range(cols_size)]
            blocks[k] = lax.ppermute(blocks[k], "col", pairs)
        steps = [0, *range(cols_size - 1, 0, -2), *range(2, cols_size, 2)]
        out = pl.pallas_call(
            functools.partial(join_kernel, steps, cols_size),
            out_shape=jax.ShapeDtypeStruct((cols_size, local_rows, out_cols), jnp.float32),
            in_specs=[pl.BlockSpec(memory_space=pltpu.VMEM)] * cols_size,
            out_specs=pl.BlockSpec(memory_space=pl.ANY),
            scratch_shapes=[pltpu.SemaphoreType.DMA((cols_size,))],
            compiler_params=pltpu.CompilerParams(vmem_limit_bytes=4 * 1024 * 1024),
        )(*[blocks[k] for k in steps])
        return out.reshape((cols_size * local_rows, out_cols))

    return per_device


def solution(mesh):
    in_specs = (P(("row", "col"), None), P(None, "row", "col"), P())
    out_specs = P("row", "col")
    per_device = make_per_device(mesh.shape["row"], mesh.shape["col"])
    return jax.shard_map(
        per_device, mesh=mesh, in_specs=in_specs, out_specs=out_specs, check_vma=False
    )
```
